768 devices in a mesh: dp: 24 (over z, core), ctx: 32 (over y, x).
Axes of the slice: x: 4, y: 8, z: 12, core: 2. Of those that a mesh axis runs over, the one named last changes fastest.
Arguments:
- hidden: bfloat16 [202752, 5120], P(('dp', 'ctx')), may hold values from -6 to 6
- value_weight: bfloat16 [5120, 128], replicated, may hold values from -0.078125 to 0.078125
- queries: bfloat16 [202752, 1024], P(('dp', 'ctx'))
- keys: bfloat16 [202752, 128], P(('dp', 'ctx'))
- attn_grad: bfloat16 [202752, 1024], P(('dp', 'ctx')), may hold values from -6 to 6
- segment_ids: int32 [24, 8192], P('dp', 'ctx'), may hold values from 0 to 3, never falling along the last dimension, each value on 1 to 4096 neighbouring positions
- partner: int32 [24], replicated, may hold values from 0 to 23, as said below
Outputs:
- attn_out: bfloat16 [202752, 1024], P(('dp', 'ctx'))
- value_grad: bfloat16 [202752, 128], P(('dp', 'ctx'))
- grad_value_weight: float32 [5120, 128], P('ctx')
The draws below stay inside these ranges and needn't reach their ends.
Inputs may be any that keep to these rules, and one draw needn't show every extreme that they name: Pairs the data groups: partner[partner[g]] == g and partner[g] != g for every g.
All inputs are finite; a program needn't handle non-finite values.
Results may differ from the reference program's by a relative error of at most 0.0057.
Values may be sent and summed in bfloat16 or wider, within the bound.
No kernel may reach another device: no remote copies, remote signals or barrier semaphores. Data moves between devices by JAX's collectives and lax.ppermute only.
A program may use at most 64 MiB of HBM per device.

```python
import math
import jax
import jax.numpy as jnp
import numpy as np
from jax import lax

D = 5120
HD = 128
HQ = 8
TOK_DEV = 256
SWAP_DEV = 8
NSEG = 4
SEQ = 8192
SPARE = 256
ROWS = 202752
N_DP = 24
N_CTX = 32


def key_base(key):
    return jax.random.normal(key, (ROWS, HD), jnp.float32)


def draw_keys(key, part):
    base = key_base(key)
    return base.astype(jnp.bfloat16)


def draw_queries(key, part):
    key = jax.random.fold_in(key, 5)
    noise = jax.random.normal(key, (ROWS, HQ, HD), jnp.float32)
    return noise.reshape(ROWS, HQ * HD).astype(jnp.bfloat16)


def draw_partner(key, part):
    key = jax.random.fold_in(key, 7)
    shuffled = jax.random.permutation(key, N_DP).astype(jnp.int32)
    first_members = shuffled[0::2]
    second_members = shuffled[1::2]
    paired = jnp.zeros((N_DP,), jnp.int32).at[first_members].set(second_members)
    paired = paired.at[second_members].set(first_members)
    return paired


def levels(rng, extent, pieces, low, high):
    level, own = 1.0, jax.random.fold_in(rng, 6)
    for axis_at, blocks in pieces:
        draws = jnp.exp(jax.random.uniform(jax.random.fold_in(own, axis_at), (blocks,), jnp.float32, low / len(pieces), high / len(pieces)))
        level = level * jnp.repeat(draws, extent[axis_at] // blocks).reshape([-1 if axis == axis_at else 1 for axis in range(len(extent))])
    return level


def profile(amount, total, bound, lean):
    weights = [(1 << 20) // math.isqrt(grade ** lean) + 1 for grade in range(2, amount + 1)]
    spare, holding = total - bound - (amount - 1), [1] * (amount - 1)
    while spare > 0:
        movable = [i for i in range(amount - 1) if holding[i] < bound]
        pool, remaining = sum([weights[i] for i in movable]), spare
        for i in movable:
            extra = min(bound - holding[i], max(1, remaining * weights[i] // pool), spare)
            holding[i] = holding[i] + extra
            spare = spare - extra
    return np.array([bound] + holding)


def ragged(stream_key, amount, total, bound, lean):
    if amount == 2:
        one = jax.random.randint(stream_key, (), max(1, total - bound), min(bound, total - 1) + 1)
        return jnp.stack([one, total - one])
    sizes = jnp.asarray(profile(amount, total, bound, lean), jnp.int32)
    twos = (amount - 1) // 2
    donor, sink = sizes[1:1 + 2 * twos:2], sizes[2:2 + 2 * twos:2]
    slack = jnp.minimum(donor - 1, bound - sink)
    passed = jax.random.randint(jax.random.fold_in(stream_key, 1), (twos,), 0, 1 << 20) % (slack + 1)
    sizes = sizes.at[1:1 + 2 * twos:2].set(donor - passed).at[2:2 + 2 * twos:2].set(sink + passed)
    return sizes[jax.random.permutation(jax.random.fold_in(stream_key, 2), amount)]


def bell_draw(stream_key, dims, spread, limit, split=(), kind=jnp.bfloat16):
    drawn = jax.random.normal(stream_key, dims, jnp.float32) * spread
    if len(split) > 0:
        drawn = levels(stream_key, dims, split, -0.22, 0.18) * drawn
    return jnp.clip(drawn, min=-limit, max=limit).astype(kind)


def setup_inputs(seed: int = 0) -> dict:
    key_list = jax.random.split(jax.random.key(seed), 8)
    hidden = bell_draw(key_list[0], (ROWS, D), 1.0, 6.0, ((0, 768),))
    value_weight = bell_draw(key_list[1], (D, HD), D ** -0.5, 0.078125)
    queries = draw_queries(jax.random.fold_in(key_list[7], 71), 0)
    keys = draw_keys(jax.random.fold_in(key_list[7], 71), 0)
    attn_grad = bell_draw(key_list[4], (ROWS, HQ * HD), 1.0, 6.0, ((0, 768),))
    segment_ids = jax.vmap(lambda own: jnp.searchsorted(jnp.cumsum(ragged(own, NSEG, SEQ, SEQ // 2, 1)), jnp.arange(SEQ), side="right"))(jax.random.split(key_list[5], N_DP)).reshape((N_DP, SEQ)).astype(jnp.int32)
    partner = draw_partner(jax.random.fold_in(key_list[7], 71), 0)
    return {"hidden": hidden, "value_weight": value_weight, "queries": queries, "keys": keys, "attn_grad": attn_grad, "segment_ids": segment_ids, "partner": partner}


big_negative = -1e30


def attend_pack(query_rows, key_rows, value_rows, grad_rows, segments, score_scale):
    seq_len = key_rows.shape[0]
    head_count = query_rows.shape[1]
    head_width = key_rows.shape[1]
    block_rows = math.gcd(seq_len, 512)
    block_count = seq_len // block_rows

    def query_block(value_acc, block_index):
        row_begin = (block_index * block_rows).astype(jnp.int32)
        query_part = lax.dynamic_slice_in_dim(query_rows, row_begin, block_rows, 0)
        grad_part = lax.dynamic_slice_in_dim(grad_rows, row_begin, block_rows, 0)
        query_segs = lax.dynamic_slice_in_dim(segments, row_begin, block_rows, 0)
        query_pos = row_begin + jnp.arange(block_rows, dtype=jnp.int32)
        seg_begin = jnp.sum((segments < query_segs[0]).astype(jnp.int32))
        first_block = (seg_begin // block_rows).astype(jnp.int32)
        last_block = (block_index + 1).astype(jnp.int32)

        def scores_at(key_index):
            key_begin = (key_index * block_rows).astype(jnp.int32)
            key_block = lax.dynamic_slice_in_dim(key_rows, key_begin, block_rows, 0)
            seg_block = lax.dynamic_slice_in_dim(segments, key_begin, block_rows, 0)
            key_pos = key_begin + jnp.arange(block_rows, dtype=jnp.int32)
            scores = jnp.einsum('qhd,kd->hqk', query_part.astype(jnp.float32), key_block.astype(jnp.float32)) * score_scale
            allowed = (query_segs[:, None] == seg_block[None, :]) & (key_pos[None, :] <= query_pos[:, None])
            return scores, allowed[None], key_begin

        def stat_step(key_index, running):
            running_max, running_sum = running
            scores, allowed, _ = scores_at(key_index)
            new_max = jnp.maximum(running_max, jnp.max(jnp.where(allowed, scores, big_negative), axis=-1))
            running_sum = running_sum * jnp.exp(running_max - new_max) + jnp.sum(jnp.where(allowed, jnp.exp(scores - new_max[..., None]), 0.0), axis=-1)
            return new_max, running_sum

        initial = (jnp.full((head_count, block_rows), big_negative, jnp.float32), jnp.zeros((head_count, block_rows), jnp.float32))
        final_max, final_sum = lax.fori_loop(first_block, last_block, stat_step, initial)
        log_total = final_max + jnp.log(final_sum)

        def weight_step(key_index, running):
            out_acc, value_part = running
            scores, allowed, key_begin = scores_at(key_index)
            weights = jnp.where(allowed, jnp.exp(scores - log_total[..., None]), 0.0).astype(jnp.bfloat16)
            value_block = lax.dynamic_slice_in_dim(value_rows, key_begin, block_rows, 0)
            out_acc = out_acc + jnp.einsum('hqk,kd->qhd', weights.astype(jnp.float32), value_block.astype(jnp.float32))
            key_terms = jnp.einsum('hqk,qhd->kd', weights.astype(jnp.float32), grad_part.astype(jnp.float32))
            current = lax.dynamic_slice_in_dim(value_part, key_begin, block_rows, 0)
            value_part = lax.dynamic_update_slice_in_dim(value_part, current + key_terms, key_begin, 0)
            return out_acc, value_part

        out_zero = jnp.zeros((block_rows, head_count, head_width), jnp.float32)
        out_sum, value_acc = lax.fori_loop(first_block, last_block, weight_step, (out_zero, value_acc))
        return value_acc, out_sum.reshape(block_rows, head_count * head_width).astype(jnp.bfloat16)

    value_zero = jnp.zeros((seq_len, head_width), jnp.float32)
    value_sum, outputs = lax.scan(query_block, value_zero, jnp.arange(block_count, dtype=jnp.int32))
    return outputs.reshape(seq_len, head_count * head_width), value_sum.astype(jnp.bfloat16)


def attend_spare(query_rows, key_rows, value_rows, grad_rows, score_scale):
    spare_len = key_rows.shape[0]
    head_count = query_rows.shape[1]
    head_width = key_rows.shape[1]
    positions = jnp.arange(spare_len, dtype=jnp.int32)
    scores = jnp.einsum('qhd,kd->hqk', query_rows.astype(jnp.float32), key_rows.astype(jnp.float32)) * score_scale
    allowed = (positions[None, :] <= positions[:, None])[None]
    row_max = jnp.max(jnp.where(allowed, scores, big_negative), axis=-1, keepdims=True)
    log_total = row_max + jnp.log(jnp.sum(jnp.where(allowed, jnp.exp(scores - row_max), 0.0), axis=-1, keepdims=True))
    weights = jnp.where(allowed, jnp.exp(scores - log_total), 0.0).astype(jnp.bfloat16)
    outputs = jnp.einsum('hqk,kd->qhd', weights.astype(jnp.float32), value_rows.astype(jnp.float32))
    value_sum = jnp.einsum('hqk,qhd->kd', weights.astype(jnp.float32), grad_rows.astype(jnp.float32))
    return outputs.reshape(spare_len, head_count * head_width).astype(jnp.bfloat16), value_sum.astype(jnp.bfloat16)


def reference(hidden, value_weight, queries, keys, attn_grad, segment_ids, partner):
    score_scale = HD ** -0.5
    per_device = TOK_DEV + SWAP_DEV
    hidden_grid = hidden.reshape(N_DP, N_CTX, per_device, D)
    query_grid = queries.reshape(N_DP, N_CTX, per_device, HQ, HD)
    key_grid = keys.reshape(N_DP, N_CTX, per_device, HD)
    grad_grid = attn_grad.reshape(N_DP, N_CTX, per_device, HQ, HD)

    def one_group(weight_acc, group_index):
        states = lax.dynamic_index_in_dim(hidden_grid, group_index, 0, keepdims=False)
        query_all = lax.dynamic_index_in_dim(query_grid, group_index, 0, keepdims=False)
        key_all = lax.dynamic_index_in_dim(key_grid, group_index, 0, keepdims=False)
        grad_all = lax.dynamic_index_in_dim(grad_grid, group_index, 0, keepdims=False)
        segments = lax.dynamic_index_in_dim(segment_ids, group_index, 0, keepdims=False)
        main_states = states[:, :TOK_DEV].reshape(SEQ, D)
        spare_states = states[:, TOK_DEV:].reshape(SPARE, D)
        main_values = jnp.dot(main_states, value_weight, preferred_element_type=jnp.float32).astype(jnp.bfloat16)
        spare_values = jnp.dot(spare_states, value_weight, preferred_element_type=jnp.float32).astype(jnp.bfloat16)
        main_out, main_grad = attend_pack(query_all[:, :TOK_DEV].reshape(SEQ, HQ, HD), key_all[:, :TOK_DEV].reshape(SEQ, HD), main_values, grad_all[:, :TOK_DEV].reshape(SEQ, HQ, HD), segments, score_scale)
        spare_out, spare_grad = attend_spare(query_all[:, TOK_DEV:].reshape(SPARE, HQ, HD), key_all[:, TOK_DEV:].reshape(SPARE, HD), spare_values, grad_all[:, TOK_DEV:].reshape(SPARE, HQ, HD), score_scale)
        weight_acc = weight_acc + jnp.dot(main_states.T, main_grad, preferred_element_type=jnp.float32)
        weight_acc = weight_acc + jnp.dot(spare_states.T, spare_grad, preferred_element_type=jnp.float32)
        return weight_acc, (main_out, main_grad, spare_out, spare_grad)

    weight_grad, (main_out, main_grad, spare_out, spare_grad) = lax.scan(one_group, jnp.zeros((D, HD), jnp.float32), jnp.arange(N_DP, dtype=jnp.int32))
    traded_out = jnp.take(spare_out, partner, axis=0)
    traded_grad = jnp.take(spare_grad, partner, axis=0)
    attn_out = jnp.concatenate([main_out.reshape(N_DP, N_CTX, TOK_DEV, HQ * HD), traded_out.reshape(N_DP, N_CTX, SWAP_DEV, HQ * HD)], axis=2)
    value_grad = jnp.concatenate([main_grad.reshape(N_DP, N_CTX, TOK_DEV, HD), traded_grad.reshape(N_DP, N_CTX, SWAP_DEV, HD)], axis=2)
    return attn_out.reshape(ROWS, HQ * HD), value_grad.reshape(ROWS, HD), weight_grad
```

```python
import functools
import math

import jax
import jax.numpy as jnp
from jax import lax
from jax.experimental import pallas as pl
from jax.experimental.pallas import tpu as pltpu
from jax.sharding import Mesh
from jax.sharding import PartitionSpec as P

BF16 = jnp.bfloat16
F32 = jnp.float32
NEG = -1e30
BIG = 1e30

NZ, NK, NY, NX = 12, 2, 8, 4
MAX_SEG = 4096


def dot(a, b, dims):
    return lax.dot_general(a, b, (dims, ((), ())), preferred_element_type=F32)


def project_kernel(hidden_ref, weight_ref, keys_ref, ids_ref, main_ref, extra_ref):
    tok = main_ref.shape[0]
    width = keys_ref.shape[1]
    values = dot(hidden_ref[...], weight_ref[...], ((1,), (0,)))
    keys = keys_ref[...].astype(F32)
    ids = ids_ref[...]
    level = lax.broadcasted_iota(jnp.int32, (8, tok), 0)
    below = jnp.sum((jnp.broadcast_to(ids, (8, tok)) < level).astype(F32), axis=1, keepdims=True)
    counts = jnp.broadcast_to(below, (8, 2 * width))
    spare = jnp.concatenate([keys[tok:], values[tok:]], axis=1)
    main_ref[...] = jnp.concatenate([keys[:tok], values[:tok]], axis=1).astype(BF16)
    extra_ref[...] = jnp.concatenate([spare, counts], axis=0).astype(BF16)


def attend_kernel(
    place_ref,
    extra_ref,
    ids_ref,
    q_ref,
    do_ref,
    qs_ref,
    dos_ref,
    kv_ref,
    kv1_ref,
    kv2_ref,
    kv3_ref,
    out_ref,
    outs_ref,
    dv_ref,
    bias_ref,
    mask_max,
    mid_max,
    mid_shift,
    total_ref,
    acc_ref,
    p_ref,
    grad_ref,
    pack_ref,
    copy_sems,
    *,
    back,
):
    tok = ids_ref.shape[1]
    width = kv_ref.shape[1] // 2
    heads = q_ref.shape[1] // width
    rows = heads * tok
    group = NY * NX
    spare = extra_ref.shape[0] // group - 8
    spare_heads = qs_ref.shape[0]
    factor = width ** (-0.5) * math.log2(math.e)
    y_at, x_at = place_ref[0], place_ref[1]
    own = y_at * NX + x_at

    copies = []
    for s, piece in enumerate((kv_ref, kv1_ref, kv2_ref, kv3_ref)):
        column = lax.rem(x_at - s + NX, NX)
        start = jnp.where((column < x_at) & (s > 0), tok, 0)
        target = pack_ref.at[column, pl.ds(pl.multiple_of(start, tok), piece.shape[0])]
        copies.append(pltpu.make_async_copy(piece, target, copy_sems.at[s]))
    for copy in copies:
        copy.start()

    dv_ref[...] = jnp.zeros_like(dv_ref)
    mask_max[...] = jnp.full_like(mask_max, NEG)
    mid_max[...] = jnp.full_like(mid_max, NEG)
    total_ref[...] = jnp.zeros_like(total_ref)
    acc_ref[...] = jnp.zeros_like(acc_ref)

    extra = extra_ref[...].astype(F32).reshape(group, spare + 8, 2 * width)
    counts = jnp.sum(extra[:, spare:, :], axis=0)[:, :tok]
    ids = ids_ref[...]
    begin = jnp.zeros((1, tok), F32)
    for v in range(1, 4):
        begin = jnp.where(ids == v, counts[v : v + 1, :], begin)
    first = jnp.min(begin).astype(jnp.int32)
    begin = begin.astype(jnp.int32)
    in_first = begin == first

    base = (y_at - back) * NX
    last = back * NX + x_at
    low = jnp.maximum(first // tok - base, x_at)
    low = jnp.minimum(low, last)

    def set_bias(n):
        position = (base + n) * tok + lax.broadcasted_iota(jnp.int32, (tok, tok), 0)
        query = own * tok + lax.broadcasted_iota(jnp.int32, (tok, tok), 1)
        allowed = (position >= begin) & (position <= query)
        bias_ref[...] = jnp.where(allowed, 0.0, NEG)

    def chunk(n, part):
        start = pl.multiple_of(lax.div(n, NX) * tok, tok)
        return pack_ref[lax.rem(n, NX), pl.ds(start, tok), part]

    def scores(key_block, h):
        return dot(key_block, q_ref[:tok, h * width : (h + 1) * width], ((1,), (1,)))

    def fold(a):
        return a.reshape(tok // 8, 8, tok)

    def max_masked(n):
        set_bias(n)
        key_block = chunk(n, slice(0, width))
        for h in range(heads):
            at = slice(h * tok, (h + 1) * tok)
            s = scores(key_block, h) * factor + bias_ref[...]
            mask_max[:, at] = jnp.maximum(mask_max[:, at], jnp.max(fold(s), axis=0))

    def max_mid(n, carry):
        key_block = chunk(n, slice(0, width))
        for h in range(heads):
            at = slice(h * tok, (h + 1) * tok)
            s = scores(key_block, h)
            mid_max[:, at] = jnp.maximum(mid_max[:, at], jnp.max(fold(s), axis=0))
        return carry

    for copy in copies:
        copy.wait()

    pl.when(low < last)(lambda: max_masked(low))
    lax.fori_loop(low + 1, last, max_mid, 0)
    max_masked(last)
    first_rows = jnp.concatenate([in_first] * heads, axis=1)
    top = jnp.max(mask_max[...], axis=0, keepdims=True)
    mid_top = jnp.max(mid_max[...], axis=0, keepdims=True) * factor
    top = jnp.where(first_rows, jnp.maximum(top, mid_top), top)
    mask_max[...] = jnp.broadcast_to(top, mask_max.shape)
    mid_shift[...] = jnp.broadcast_to(jnp.where(first_rows, top, BIG), mid_shift.shape)

    def weigh(n, shift_ref, masked):
        key_block = chunk(n, slice(0, width))
        value_t = chunk(n, slice(width, 2 * width)).astype(F32).T.astype(BF16)
        for h in range(heads):
            at = slice(h * tok, (h + 1) * tok)
            s = scores(key_block, h) * factor
            if masked:
                s = s + bias_ref[...]
            p = jnp.exp2(s - shift_ref[0:1, at])
            total_ref[:, at] += jnp.sum(fold(p), axis=0)
            p = p.astype(BF16)
            p_ref[n - x_at, :, at] = p
            acc_ref[:, at] += dot(value_t, p, ((1,), (0,)))

    def weigh_mid(n, carry):
        weigh(n, mid_shift, False)
        return carry

    weigh(last, mask_max, True)
    lax.fori_loop(low + 1, last, weigh_mid, 0)

    @pl.when(low < last)
    def _():
        set_bias(low)
        weigh(low, mask_max, True)

    share = 1.0 / jnp.sum(total_ref[...], axis=0, keepdims=True)
    for h in range(heads):
        at = slice(h * tok, (h + 1) * tok)
        part = slice(h * width, (h + 1) * width)
        head_share = jnp.broadcast_to(share[:, at], (width, tok))
        out_ref[:tok, part] = (acc_ref[:, at] * head_share).T.astype(BF16)
        grad_ref[at, :] = (do_ref[:tok, part].astype(F32) * head_share.T).astype(BF16)

    def spread(n, carry):
        got = dot(p_ref[n - x_at], grad_ref[...], ((1,), (0,)))
        column = lax.rem(n, NX)
        row = lax.div(n, NX)
        dv_ref[column, pl.ds(pl.multiple_of(row * tok, tok), tok), :] = got.astype(BF16)
        return carry

    lax.fori_loop(low, last + 1, spread, 0)

    spare_total = group * spare
    block = extra[:, :spare, :].reshape(spare_total, 2 * width).astype(BF16)
    s = dot(block[:, :width], qs_ref[...], ((1,), (1,))) * factor
    key_at = lax.broadcasted_iota(jnp.int32, (spare_total, spare_heads), 0)
    query_at = own * spare + lax.div(
        lax.broadcasted_iota(jnp.int32, (spare_total, spare_heads), 1), heads
    )
    allowed = key_at <= query_at
    s = jnp.where(allowed, s, NEG)
    p = jnp.where(allowed, jnp.exp2(s - jnp.max(s, axis=0, keepdims=True)), 0.0)
    p = (p * (1.0 / jnp.sum(p, axis=0, keepdims=True))).astype(BF16)
    outs_ref[...] = dot(p, block[:, width:], ((0,), (0,))).astype(BF16)
    got = dot(p, dos_ref[...], ((1,), (0,))).reshape(NY, NX, spare, width)
    for xx in range(NX):
        dv_ref[xx, (back + 1) * tok :, :] = got[:, xx].reshape(NY * spare, width).astype(BF16)


VMEM = pl.BlockSpec(memory_space=pltpu.VMEM)
SMEM = pl.BlockSpec(memory_space=pltpu.SMEM)
LIMIT = pltpu.CompilerParams(vmem_limit_bytes=50 * 1024 * 1024)


def project(hidden, value_weight, keys, segment_ids):
    tok = segment_ids.shape[1]
    width = keys.shape[1]
    return pl.pallas_call(
        project_kernel,
        out_shape=(
            jax.ShapeDtypeStruct((tok, 2 * width), BF16),
            jax.ShapeDtypeStruct((16, 2 * width), BF16),
        ),
        in_specs=[VMEM] * 4,
        out_specs=(VMEM, VMEM),
        compiler_params=LIMIT,
        name="project",
    )(hidden, value_weight, keys, segment_ids)


def attend(place, extra, segment_ids, queries, attn_grad, spare_q, spare_do, pieces, back):
    tok = segment_ids.shape[1]
    width = pieces[0].shape[1] // 2
    heads = queries.shape[1] // width
    spare = extra.shape[0] // (NY * NX) - 8
    rows = heads * tok
    return pl.pallas_call(
        functools.partial(attend_kernel, back=back),
        out_shape=(
            jax.ShapeDtypeStruct(queries.shape, BF16),
            jax.ShapeDtypeStruct(spare_q.shape, BF16),
            jax.ShapeDtypeStruct((NX, (back + 1) * tok + NY * spare, width), BF16),
        ),
        in_specs=[SMEM] + [VMEM] * 6 + [pl.BlockSpec(memory_space=pl.ANY)] * NX,
        out_specs=(VMEM, VMEM, VMEM),
        scratch_shapes=[
            pltpu.VMEM((tok, tok), F32),
            pltpu.VMEM((8, rows), F32),
            pltpu.VMEM((8, rows), F32),
            pltpu.VMEM((8, rows), F32),
            pltpu.VMEM((8, rows), F32),
            pltpu.VMEM((width, rows), F32),
            pltpu.VMEM((back * NX + 1, tok, rows), BF16),
            pltpu.VMEM((rows, width), BF16),
            pltpu.VMEM((NX, (back + 1) * tok, 2 * width), BF16),
            pltpu.SemaphoreType.DMA((NX,)),
        ],
        compiler_params=LIMIT,
        name="attend",
    )(place, extra, segment_ids, queries, attn_grad, spare_q, spare_do, *pieces)


def shift(array, axis, size, step):
    return lax.ppermute(array, axis, [(i, (i + step) % size) for i in range(size)])


def body(hidden, value_weight, queries, keys, attn_grad, segment_ids, partner):
    tok = segment_ids.shape[1]
    spare = hidden.shape[0] - tok
    width = keys.shape[1]
    heads = queries.shape[1] // width
    back = MAX_SEG // (tok * NX)
    y_at, x_at, k_at = lax.axis_index("y"), lax.axis_index("x"), lax.axis_index("k")

    main, extra = project(hidden, value_weight, keys, segment_ids)
    spare_q = queries[tok:].reshape(spare * heads, width)
    spare_do = attn_grad[tok:].reshape(spare * heads, width)

    rows = [shift(main, "y", NY, k) for k in range(back, 0, -1)] + [main]
    extras = lax.all_to_all(
        jnp.broadcast_to(extra[None], (NY * NX,) + extra.shape), ("y", "x"), 0, 0, tiled=True
    ).reshape(NY * NX * extra.shape[0], 2 * width)
    column = jnp.concatenate(rows, axis=0)
    early, late = column[: back * tok], column[tok:]
    pieces = [column]
    for s in range(1, NX):
        send = jnp.where(x_at + s < NX, late, early)
        pieces.append(shift(send, "x", NX, s))

    place = jnp.stack([y_at, x_at]).astype(jnp.int32)
    main_out, spare_out, sums = attend(
        place, extras, segment_ids, queries, attn_grad, spare_q, spare_do, pieces, back
    )

    got = lax.all_to_all(sums, "x", 0, 0, tiled=True)
    got = jnp.sum(got.astype(F32), axis=0).astype(BF16)
    main_part = got[: (back + 1) * tok].reshape(back + 1, tok, width)
    main_part = jnp.concatenate(
        [main_part, jnp.zeros((NY - back - 1, tok, width), BF16)], axis=0
    )
    main_part = jnp.concatenate([main_part, main_part], axis=0)
    main_part = lax.dynamic_slice_in_dim(main_part, (back - y_at + NY) % NY, NY, 0)
    spare_part = got[(back + 1) * tok :].reshape(NY, spare, width)
    got = lax.all_to_all(jnp.concatenate([main_part, spare_part], axis=1), "y", 0, 0, tiled=True)
    home = jnp.sum(got.astype(F32), axis=0).astype(BF16)

    term = dot(hidden, home, ((0,), (0,))).reshape(NY * NX, NK, -1, width)
    mine = lax.dynamic_index_in_dim(term, k_at, 1, keepdims=False)
    other = lax.dynamic_index_in_dim(term, 1 - k_at, 1, keepdims=False).astype(BF16)
    both = (mine + shift(other, "k", NK, 1).astype(F32)).astype(BF16)
    got = lax.all_to_all(both, ("y", "x"), 0, 0, tiled=True)
    share = jnp.sum(got.astype(F32), axis=0).astype(BF16)

    bundle = jnp.concatenate([share, home[tok:], spare_out], axis=0)
    every = lax.all_gather(bundle, ("z", "k"), axis=0)
    count = share.shape[0]
    weight_grad = jnp.sum(
        every[:, :count].astype(F32).reshape(NZ, NK * count, width), axis=0
    )
    my_partner = partner[lax.axis_index("z") * NK + k_at]
    traded = lax.dynamic_index_in_dim(every[:, count:], my_partner, 0, keepdims=False)
    attn_out = lax.dynamic_update_slice(
        main_out, traded[spare:].reshape(spare, heads * width), (tok, 0)
    )
    value_grad = jnp.concatenate([home[:tok], traded[:spare]], axis=0)
    return (attn_out, value_grad, weight_grad)


def solution(mesh):
    grid = Mesh(mesh.devices.reshape(NZ, NK, NY, NX), ("z", "k", "y", "x"))
    everywhere = P(("z", "k", "y", "x"), None)
    placed = (
        everywhere,
        P(),
        everywhere,
        everywhere,
        everywhere,
        P(("z", "k"), ("y", "x")),
        P(),
    )
    return jax.shard_map(
        body,
        mesh=grid,
        in_specs=placed,
        out_specs=(everywhere, everywhere, P(("y", "x"), None)),
        check_vma=False,
    )
```

```python
import functools
import math

import jax
import jax.numpy as jnp
from jax import lax
from jax.experimental import pallas as pl
from jax.experimental.pallas import tpu as pltpu
from jax.sharding import Mesh
from jax.sharding import PartitionSpec as P

BF16 = jnp.bfloat16
F32 = jnp.float32
NEG = -1e30
BIG = 1e30

NZ, NK, NY, NX = 12, 2, 8, 4
MAX_SEG = 4096
SAFE = 40.0
MARGIN = 1.02


def dot(a, b, dims):
    return lax.dot_general(a, b, (dims, ((), ())), preferred_element_type=F32)


def project_kernel(hidden_ref, weight_ref, keys_ref, ids_ref, main_ref, extra_ref):
    tok = main_ref.shape[0]
    width = keys_ref.shape[1]
    values = dot(hidden_ref[...], weight_ref[...], ((1,), (0,)))
    keys = keys_ref[...].astype(F32)
    ids = ids_ref[...]
    level = lax.broadcasted_iota(jnp.int32, (8, tok), 0)
    below = jnp.sum((jnp.broadcast_to(ids, (8, tok)) < level).astype(F32), axis=1, keepdims=True)
    longest = jnp.max(jnp.sum(keys * keys, axis=1, keepdims=True)) * MARGIN
    line = lax.broadcasted_iota(jnp.int32, (8, 1), 0)
    counts = jnp.broadcast_to(jnp.where(line == 4, longest, below), (8, 2 * width))
    spare = jnp.concatenate([keys[tok:], values[tok:]], axis=1)
    main_ref[...] = jnp.concatenate([keys[:tok], values[:tok]], axis=1).astype(BF16)
    extra_ref[...] = jnp.concatenate([spare, counts], axis=0).astype(BF16)


def attend_kernel(
    place_ref,
    extra_ref,
    ids_ref,
    q_ref,
    do_ref,
    qs_ref,
    dos_ref,
    kv_ref,
    kv1_ref,
    kv2_ref,
    kv3_ref,
    out_ref,
    outs_ref,
    dv_ref,
    bias_ref,
    mask_max,
    mid_max,
    mid_shift,
    total_ref,
    acc_ref,
    p_ref,
    grad_ref,
    pack_ref,
    copy_sems,
    *,
    back,
):
    tok = ids_ref.shape[1]
    width = kv_ref.shape[1] // 2
    heads = q_ref.shape[1] // width
    rows = heads * tok
    group = NY * NX
    spare = extra_ref.shape[0] // group - 8
    spare_heads = qs_ref.shape[0]
    factor = width ** (-0.5) * math.log2(math.e)
    y_at, x_at = place_ref[0], place_ref[1]
    own = y_at * NX + x_at

    copies = []
    for s, piece in enumerate((kv_ref, kv1_ref, kv2_ref, kv3_ref)):
        column = lax.rem(x_at - s + NX, NX)
        start = jnp.where((column < x_at) & (s > 0), tok, 0)
        target = pack_ref.at[column, pl.ds(pl.multiple_of(start, tok), piece.shape[0])]
        copies.append(pltpu.make_async_copy(piece, target, copy_sems.at[s]))
    for copy in copies:
        copy.start()

    dv_ref[...] = jnp.zeros_like(dv_ref)
    total_ref[...] = jnp.zeros_like(total_ref)
    acc_ref[...] = jnp.zeros_like(acc_ref)

    extra = extra_ref[...].astype(F32).reshape(group, spare + 8, 2 * width)
    counts = jnp.sum(extra[:, spare:, :], axis=0)[:, :tok]
    ids = ids_ref[...]
    begin = jnp.zeros((1, tok), F32)
    for v in range(1, 4):
        begin = jnp.where(ids == v, counts[v : v + 1, :], begin)
    first = jnp.min(begin).astype(jnp.int32)
    begin = begin.astype(jnp.int32)
    in_first = begin == first
    first_rows = jnp.concatenate([in_first] * heads, axis=1)
    key_bound = jnp.max(extra[:, spare + 4, :])
    ones = jnp.ones((width, width), BF16)
    lengths = []
    for h in range(heads):
        part = q_ref[:tok, h * width : (h + 1) * width].astype(F32)
        lengths.append(jnp.max(dot((part * part).astype(BF16), ones, ((1,), (0,))), axis=0, keepdims=True))
    query_bound = jnp.max(jnp.concatenate(lengths, axis=0)) * MARGIN
    safe = key_bound * query_bound <= SAFE * SAFE * width

    base = (y_at - back) * NX
    last = back * NX + x_at
    low = jnp.maximum(first // tok - base, x_at)
    low = jnp.minimum(low, last)

    def set_bias(n):
        position = (base + n) * tok + lax.broadcasted_iota(jnp.int32, (tok, tok), 0)
        query = own * tok + lax.broadcasted_iota(jnp.int32, (tok, tok), 1)
        allowed = (position >= begin) & (position <= query)
        bias_ref[...] = jnp.where(allowed, 0.0, NEG)

    def chunk(n, part):
        start = pl.multiple_of(lax.div(n, NX) * tok, tok)
        return pack_ref[lax.rem(n, NX), pl.ds(start, tok), part]

    def scores(key_block, h):
        return dot(key_block, q_ref[:tok, h * width : (h + 1) * width], ((1,), (1,)))

    def fold(a):
        return a.reshape(tok // 8, 8, tok)

    def max_masked(n):
        set_bias(n)
        key_block = chunk(n, slice(0, width))
        for h in range(heads):
            at = slice(h * tok, (h + 1) * tok)
            s = scores(key_block, h) * factor + bias_ref[...]
            mask_max[:, at] = jnp.maximum(mask_max[:, at], jnp.max(fold(s), axis=0))

    def max_mid(n, carry):
        key_block = chunk(n, slice(0, width))
        for h in range(heads):
            at = slice(h * tok, (h + 1) * tok)
            s = scores(key_block, h)
            mid_max[:, at] = jnp.maximum(mid_max[:, at], jnp.max(fold(s), axis=0))
        return carry

    for copy in copies:
        copy.wait()

    def set_shift(top):
        mask_max[...] = jnp.broadcast_to(top, mask_max.shape)
        mid_shift[...] = jnp.broadcast_to(jnp.where(first_rows, top, BIG), mid_shift.shape)

    @pl.when(safe)
    def _():
        set_shift(jnp.zeros((1, rows), F32))

    @pl.when(jnp.logical_not(safe))
    def _():
        mask_max[...] = jnp.full_like(mask_max, NEG)
        mid_max[...] = jnp.full_like(mid_max, NEG)
        pl.when(low < last)(lambda: max_masked(low))
        lax.fori_loop(low + 1, last, max_mid, 0)
        max_masked(last)
        top = jnp.max(mask_max[...], axis=0, keepdims=True)
        mid_top = jnp.max(mid_max[...], axis=0, keepdims=True) * factor
        set_shift(jnp.where(first_rows, jnp.maximum(top, mid_top), top))

    def weigh(n, shift_ref, masked):
        key_block = chunk(n, slice(0, width))
        for h in range(heads):
            at = slice(h * tok, (h + 1) * tok)
            s = scores(key_block, h) * factor
            if masked:
                s = s + bias_ref[...]
            p = jnp.exp2(s - shift_ref[0:1, at])
            total_ref[:, at] += jnp.sum(fold(p), axis=0)
            p_ref[n - low, :, at] = p.astype(BF16)

    def weigh_mid(n, carry):
        weigh(n, mid_shift, False)
        return carry

    set_bias(last)
    weigh(last, mask_max, True)
    lax.fori_loop(low + 1, last, weigh_mid, 0)

    @pl.when(low < last)
    def _():
        set_bias(low)
        weigh(low, mask_max, True)

    p_ref[last - low + 1] = jnp.zeros((tok, rows), BF16)

    def gather_values(j, carry):
        near = low + 2 * j
        block = [chunk(n, slice(width, 2 * width)) for n in (near, jnp.minimum(near + 1, last))]
        value_t = jnp.concatenate([b.astype(F32).T.astype(BF16) for b in block], axis=1)
        weights = p_ref[pl.ds(2 * j, 2)].reshape(2 * tok, rows)
        acc_ref[...] += dot(value_t, weights, ((1,), (0,)))
        return carry

    lax.fori_loop(0, lax.div(last - low + 2, 2), gather_values, 0)

    share = 1.0 / jnp.sum(total_ref[...], axis=0, keepdims=True)
    for h in range(heads):
        at = slice(h * tok, (h + 1) * tok)
        part = slice(h * width, (h + 1) * width)
        head_share = jnp.broadcast_to(share[:, at], (width, tok))
        out_ref[:tok, part] = (acc_ref[:, at] * head_share).T.astype(BF16)
        grad_ref[at, :] = (do_ref[:tok, part].astype(F32) * head_share.T).astype(BF16)

    def spread(n, carry):
        got = dot(p_ref[n - low], grad_ref[...], ((1,), (0,)))
        column = lax.rem(n, NX)
        row = lax.div(n, NX)
        dv_ref[column, pl.ds(pl.multiple_of(row * tok, tok), tok), :] = got.astype(BF16)
        return carry

    lax.fori_loop(low, last + 1, spread, 0)

    spare_total = group * spare
    block = extra[:, :spare, :].reshape(spare_total, 2 * width).astype(BF16)
    s = dot(block[:, :width], qs_ref[...], ((1,), (1,))) * factor
    key_at = lax.broadcasted_iota(jnp.int32, (spare_total, spare_heads), 0)
    query_at = own * spare + lax.div(
        lax.broadcasted_iota(jnp.int32, (spare_total, spare_heads), 1), heads
    )
    allowed = key_at <= query_at
    s = jnp.where(allowed, s, NEG)
    p = jnp.where(allowed, jnp.exp2(s - jnp.max(s, axis=0, keepdims=True)), 0.0)
    p = (p * (1.0 / jnp.sum(p, axis=0, keepdims=True))).astype(BF16)
    outs_ref[...] = dot(p, block[:, width:], ((0,), (0,))).astype(BF16)
    got = dot(p, dos_ref[...], ((1,), (0,))).reshape(NY, NX, spare, width)
    for xx in range(NX):
        dv_ref[xx, (back + 1) * tok :, :] = got[:, xx].reshape(NY * spare, width).astype(BF16)


def combine_kernel(place_ref, got_ref, hidden_ref, home_ref, mine_ref, other_ref):
    home = jnp.sum(got_ref[...].astype(F32), axis=0)
    home_ref[...] = home.astype(BF16)
    home = home.astype(BF16)
    first = place_ref[2] == 0
    half = mine_ref.shape[1]
    step = 4
    for c in range(0, NY * NX, step):
        columns = slice(2 * half * c, 2 * half * (c + step))
        term = dot(hidden_ref[:, columns], home, ((0,), (0,)))
        term = term.reshape(step, NK, half, home.shape[1])
        mine_ref[c : c + step] = jnp.where(first, term[:, 0], term[:, 1])
        other_ref[c : c + step] = jnp.where(first, term[:, 1], term[:, 0])


VMEM = pl.BlockSpec(memory_space=pltpu.VMEM)
SMEM = pl.BlockSpec(memory_space=pltpu.SMEM)
LIMIT = pltpu.CompilerParams(vmem_limit_bytes=50 * 1024 * 1024)


def project(hidden, value_weight, keys, segment_ids):
    tok = segment_ids.shape[1]
    width = keys.shape[1]
    return pl.pallas_call(
        project_kernel,
        out_shape=(
            jax.ShapeDtypeStruct((tok, 2 * width), BF16),
            jax.ShapeDtypeStruct((16, 2 * width), BF16),
        ),
        in_specs=[VMEM] * 4,
        out_specs=(VMEM, VMEM),
        compiler_params=LIMIT,
        name="project",
    )(hidden, value_weight, keys, segment_ids)


def attend(place, extra, segment_ids, queries, attn_grad, spare_q, spare_do, pieces, back):
    tok = segment_ids.shape[1]
    width = pieces[0].shape[1] // 2
    heads = queries.shape[1] // width
    spare = extra.shape[0] // (NY * NX) - 8
    rows = heads * tok
    return pl.pallas_call(
        functools.partial(attend_kernel, back=back),
        out_shape=(
            jax.ShapeDtypeStruct(queries.shape, BF16),
            jax.ShapeDtypeStruct(spare_q.shape, BF16),
            jax.ShapeDtypeStruct((NX, (back + 1) * tok + NY * spare, width), BF16),
        ),
        in_specs=[SMEM] + [VMEM] * 6 + [pl.BlockSpec(memory_space=pl.ANY)] * NX,
        out_specs=(VMEM, VMEM, VMEM),
        scratch_shapes=[
            pltpu.VMEM((tok, tok), F32),
            pltpu.VMEM((8, rows), F32),
            pltpu.VMEM((8, rows), F32),
            pltpu.VMEM((8, rows), F32),
            pltpu.VMEM((8, rows), F32),
            pltpu.VMEM((width, rows), F32),
            pltpu.VMEM((back * NX + 2, tok, rows), BF16),
            pltpu.VMEM((rows, width), BF16),
            pltpu.VMEM((NX, (back + 1) * tok, 2 * width), BF16),
            pltpu.SemaphoreType.DMA((NX,)),
        ],
        compiler_params=LIMIT,
        name="attend",
    )(place, extra, segment_ids, queries, attn_grad, spare_q, spare_do, *pieces)


def combine(place, got, hidden):
    share = hidden.shape[1] // (NY * NX * NK)
    width = got.shape[2]
    part = jax.ShapeDtypeStruct((NY * NX, share, width), F32)
    return pl.pallas_call(
        combine_kernel,
        out_shape=(jax.ShapeDtypeStruct(got.shape[1:], BF16), part, part),
        in_specs=[SMEM, VMEM, VMEM],
        out_specs=(VMEM, VMEM, VMEM),
        compiler_params=LIMIT,
        name="combine",
    )(place, got, hidden)


def shift(array, axis, size, step):
    return lax.ppermute(array, axis, [(i, (i + step) % size) for i in range(size)])


def body(hidden, value_weight, queries, keys, attn_grad, segment_ids, partner):
    tok = segment_ids.shape[1]
    spare = hidden.shape[0] - tok
    width = keys.shape[1]
    heads = queries.shape[1] // width
    back = MAX_SEG // (tok * NX)
    y_at, x_at, k_at = lax.axis_index("y"), lax.axis_index("x"), lax.axis_index("k")

    main, extra = project(hidden, value_weight, keys, segment_ids)
    spare_q = queries[tok:].reshape(spare * heads, width)
    spare_do = attn_grad[tok:].reshape(spare * heads, width)

    rows = [shift(main, "y", NY, k) for k in range(back, 0, -1)] + [main]
    extras = lax.all_to_all(
        jnp.broadcast_to(extra[None], (NY * NX,) + extra.shape), ("y", "x"), 0, 0, tiled=True
    ).reshape(NY * NX * extra.shape[0], 2 * width)
    column = jnp.concatenate(rows, axis=0)
    early, late = column[: back * tok], column[tok:]
    pieces = [column]
    for s in range(1, NX):
        send = jnp.where(x_at + s < NX, late, early)
        pieces.append(shift(send, "x", NX, s))

    place = jnp.stack([y_at, x_at, k_at]).astype(jnp.int32)
    main_out, spare_out, sums = attend(
        place, extras, segment_ids, queries, attn_grad, spare_q, spare_do, pieces, back
    )

    got = lax.all_to_all(sums, "x", 0, 0, tiled=True)
    got = jnp.sum(got.astype(F32), axis=0).astype(BF16)
    main_part = got[: (back + 1) * tok].reshape(back + 1, tok, width)
    main_part = jnp.concatenate(
        [main_part, jnp.zeros((NY - back - 1, tok, width), BF16)], axis=0
    )
    main_part = jnp.concatenate([main_part, main_part], axis=0)
    main_part = lax.dynamic_slice_in_dim(main_part, (back - y_at + NY) % NY, NY, 0)
    spare_part = got[(back + 1) * tok :].reshape(NY, spare, width)
    got = lax.all_to_all(jnp.concatenate([main_part, spare_part], axis=1), "y", 0, 0, tiled=True)
    home, mine, other = combine(place, got, hidden)
    both = (mine + shift(other, "k", NK, 1)).astype(BF16)
    got = lax.all_to_all(both, ("y", "x"), 0, 0, tiled=True)
    share = jnp.sum(got.astype(F32), axis=0).astype(BF16)

    bundle = jnp.concatenate([share, home[tok:], spare_out], axis=0)
    every = lax.all_gather(bundle, ("z", "k"), axis=0)
    count = share.shape[0]
    weight_grad = jnp.sum(
        every[:, :count].astype(F32).reshape(NZ, NK * count, width), axis=0
    )
    my_partner = partner[lax.axis_index("z") * NK + k_at]
    traded = lax.dynamic_index_in_dim(every[:, count:], my_partner, 0, keepdims=False)
    attn_out = lax.dynamic_update_slice(
        main_out, traded[spare:].reshape(spare, heads * width), (tok, 0)
    )
    value_grad = jnp.concatenate([home[:tok], traded[:spare]], axis=0)
    return (attn_out, value_grad, weight_grad)


def solution(mesh):
    grid = Mesh(mesh.devices.reshape(NZ, NK, NY, NX), ("z", "k", "y", "x"))
    everywhere = P(("z", "k", "y", "x"), None)
    placed = (
        everywhere,
        P(),
        everywhere,
        everywhere,
        everywhere,
        P(("z", "k"), ("y", "x")),
        P(),
    )
    return jax.shard_map(
        body,
        mesh=grid,
        in_specs=placed,
        out_specs=(everywhere, everywhere, P(("y", "x"), None)),
        check_vma=False,
    )
```

```python
import functools
import math

import jax
import jax.numpy as jnp
from jax import lax
from jax.experimental import pallas as pl
from jax.experimental.pallas import tpu as pltpu
from jax.sharding import Mesh
from jax.sharding import PartitionSpec as P

BF16 = jnp.bfloat16
F32 = jnp.float32
NEG = -1e30
BIG = 1e30

NZ, NK, NY, NX = 12, 2, 8, 4
MAX_SEG = 4096
SAFE = 40.0
MARGIN = 1.02


def dot(a, b, dims):
    return lax.dot_general(a, b, (dims, ((), ())), preferred_element_type=F32)


def project_kernel(hidden_ref, weight_ref, keys_ref, ids_ref, out_ref, sum_ref):
    step = pl.program_id(0)
    part = dot(hidden_ref[...], weight_ref[...], ((1,), (0,)))

    @pl.when(step == 0)
    def _():
        sum_ref[...] = part

    @pl.when(step > 0)
    def _():
        sum_ref[...] += part

    @pl.when(step == pl.num_programs(0) - 1)
    def _():
        tok = ids_ref.shape[1]
        width = keys_ref.shape[1]
        values = sum_ref[...]
        keys = keys_ref[...].astype(F32)
        ids = jnp.broadcast_to(ids_ref[...], (8, tok))
        level = lax.broadcasted_iota(jnp.int32, (8, tok), 0)
        below = jnp.sum((ids < level).astype(F32), axis=1, keepdims=True)
        longest = jnp.max(jnp.sum(keys * keys, axis=1, keepdims=True)) * MARGIN
        line = lax.broadcasted_iota(jnp.int32, (8, 1), 0)
        counts = jnp.broadcast_to(jnp.where(line == 4, longest, below), (8, 2 * width))
        spare = jnp.concatenate([keys[tok:], values[tok:]], axis=1)
        main = jnp.concatenate([keys[:tok], values[:tok]], axis=1).astype(BF16)
        main = main.reshape(tok // 16, 16, 2 * width)
        extra = jnp.concatenate([spare, counts], axis=0).astype(BF16)
        for i in range(out_ref.shape[0]):
            out_ref[i, : tok // 16] = main
            out_ref[i, tok // 16] = extra


def select_kernel(place_ref, got_ref, one_ref, two_ref, three_ref, *, back):
    y_at, x_at = place_ref[0], place_ref[1]
    blocks = got_ref.shape[1] - 1
    for s, send_ref in enumerate((one_ref, two_ref, three_ref)):
        late = jnp.where(x_at + s + 1 < NX, 1, 0)
        for r in range(back):
            row = lax.rem(y_at - back + r + late + NY, NY)
            send_ref[r * blocks : (r + 1) * blocks] = got_ref[row, :blocks]
        for i in range(NY):
            send_ref[back * blocks + i] = got_ref[i, blocks]


def attend_kernel(
    place_ref,
    ids_ref,
    q_ref,
    do_ref,
    qs_ref,
    dos_ref,
    kv_ref,
    one_ref,
    two_ref,
    three_ref,
    out_ref,
    outs_ref,
    dv_ref,
    bias_ref,
    mask_max,
    mid_max,
    mid_shift,
    total_ref,
    acc_ref,
    p_ref,
    grad_ref,
    pack_ref,
    extra_ref,
    copy_sems,
    *,
    back,
):
    tok = ids_ref.shape[1]
    width = kv_ref.shape[3] // 2
    heads = q_ref.shape[1] // width
    rows = heads * tok
    group = NY * NX
    spare = 8
    blocks = tok // 16
    spare_heads = qs_ref.shape[0]
    factor = width ** (-0.5) * math.log2(math.e)
    y_at, x_at = place_ref[0], place_ref[1]
    own = y_at * NX + x_at

    copies = []

    def fetch(source, target):
        copies.append(pltpu.make_async_copy(source, target, copy_sems.at[len(copies)]))

    for s, piece in enumerate((one_ref, two_ref, three_ref)):
        column = lax.rem(x_at - s - 1 + NX, NX)
        start = jnp.where(column < x_at, blocks, 0)
        start = pl.multiple_of(start, blocks)
        fetch(piece.at[back * blocks :], extra_ref.at[column])
        fetch(piece.at[: back * blocks], pack_ref.at[column, pl.ds(start, back * blocks)])
    fetch(kv_ref.at[:, blocks], extra_ref.at[x_at])
    for r in range(back + 1):
        row = lax.rem(y_at - back + r + NY, NY)
        fetch(
            kv_ref.at[row, :blocks],
            pack_ref.at[x_at, r * blocks : (r + 1) * blocks],
        )
    for copy in copies:
        copy.start()

    dv_ref[...] = jnp.zeros_like(dv_ref)
    total_ref[...] = jnp.zeros_like(total_ref)
    acc_ref[...] = jnp.zeros_like(acc_ref)

    ones = jnp.ones((width, width), BF16)
    lengths = []
    for h in range(heads):
        part = q_ref[:tok, h * width : (h + 1) * width].astype(F32)
        lengths.append(jnp.max(dot((part * part).astype(BF16), ones, ((1,), (0,))), axis=0, keepdims=True))
    query_bound = jnp.max(jnp.concatenate(lengths, axis=0)) * MARGIN
    for copy in copies:
        copy.wait()

    extra = extra_ref[...].astype(F32).reshape(group, spare + 8, 2 * width)
    counts = jnp.sum(extra[:, spare:, :], axis=0)[:, :tok]
    ids = ids_ref[...]
    begin = jnp.zeros((1, tok), F32)
    for v in range(1, 4):
        begin = jnp.where(ids == v, counts[v : v + 1, :], begin)
    first = jnp.min(begin).astype(jnp.int32)
    begin = begin.astype(jnp.int32)
    in_first = begin == first
    first_rows = jnp.concatenate([in_first] * heads, axis=1)
    key_bound = jnp.max(extra[:, spare + 4, :])
    safe = key_bound * query_bound <= SAFE * SAFE * width

    base = (y_at - back) * NX
    last = back * NX + x_at
    low = jnp.maximum(first // tok - base, x_at)
    low = jnp.minimum(low, last)

    def set_bias(n):
        position = (base + n) * tok + lax.broadcasted_iota(jnp.int32, (tok, tok), 0)
        query = own * tok + lax.broadcasted_iota(jnp.int32, (tok, tok), 1)
        allowed = (position >= begin) & (position <= query)
        bias_ref[...] = jnp.where(allowed, 0.0, NEG)

    def chunk(n, part):
        start = pl.multiple_of(lax.div(n, NX) * blocks, blocks)
        return pack_ref[lax.rem(n, NX), pl.ds(start, blocks), :, part].reshape(tok, width)

    def scores(key_block, h):
        return dot(key_block, q_ref[:tok, h * width : (h + 1) * width], ((1,), (1,)))

    def fold(a):
        return a.reshape(tok // 8, 8, tok)

    def max_masked(n):
        set_bias(n)
        key_block = chunk(n, slice(0, width))
        for h in range(heads):
            at = slice(h * tok, (h + 1) * tok)
            s = scores(key_block, h) * factor + bias_ref[...]
            mask_max[:, at] = jnp.maximum(mask_max[:, at], jnp.max(fold(s), axis=0))

    def max_mid(n, carry):
        key_block = chunk(n, slice(0, width))
        for h in range(heads):
            at = slice(h * tok, (h + 1) * tok)
            s = scores(key_block, h)
            mid_max[:, at] = jnp.maximum(mid_max[:, at], jnp.max(fold(s), axis=0))
        return carry

    def set_shift(top):
        mask_max[...] = jnp.broadcast_to(top, mask_max.shape)
        mid_shift[...] = jnp.broadcast_to(jnp.where(first_rows, top, BIG), mid_shift.shape)

    @pl.when(safe)
    def _():
        set_shift(jnp.zeros((1, rows), F32))

    @pl.when(jnp.logical_not(safe))
    def _():
        mask_max[...] = jnp.full_like(mask_max, NEG)
        mid_max[...] = jnp.full_like(mid_max, NEG)
        pl.when(low < last)(lambda: max_masked(low))
        lax.fori_loop(low + 1, last, max_mid, 0)
        max_masked(last)
        top = jnp.max(mask_max[...], axis=0, keepdims=True)
        mid_top = jnp.max(mid_max[...], axis=0, keepdims=True) * factor
        set_shift(jnp.where(first_rows, jnp.maximum(top, mid_top), top))

    def weigh_masked(n):
        key_block = chunk(n, slice(0, width))
        for h in range(heads):
            at = slice(h * tok, (h + 1) * tok)
            s = scores(key_block, h) * factor + bias_ref[...]
            p = jnp.exp2(s - mask_max[0:1, at])
            total_ref[:, at] += jnp.sum(fold(p), axis=0)
            p_ref[n - low, :, at] = p.astype(BF16)

    def weigh_mid(n, count):
        key_block = [chunk(n + i, slice(0, width)) for i in range(count)]
        key_block = jnp.concatenate(key_block, axis=0)
        for h in range(heads):
            at = slice(h * tok, (h + 1) * tok)
            p = jnp.exp2(scores(key_block, h) * factor - mid_shift[0:1, at])
            total_ref[:, at] += jnp.sum(p.reshape(count * tok // 8, 8, tok), axis=0)
            p_ref[pl.ds(n - low, count), :, at] = p.astype(BF16).reshape(count, tok, tok)

    def weigh_two(j, carry):
        weigh_mid(low + 1 + 2 * j, 2)
        return carry

    set_bias(last)
    weigh_masked(last)
    mid_count = jnp.maximum(last - low - 1, 0)
    lax.fori_loop(0, lax.div(mid_count, 2), weigh_two, 0)
    pl.when(lax.rem(mid_count, 2) == 1)(lambda: weigh_mid(last - 1, 1))

    @pl.when(low < last)
    def _():
        set_bias(low)
        weigh_masked(low)

    share = 1.0 / jnp.sum(total_ref[...], axis=0, keepdims=True)
    for h in range(heads):
        at = slice(h * tok, (h + 1) * tok)
        part = slice(h * width, (h + 1) * width)
        head_share = jnp.broadcast_to(share[:, at], (width, tok)).T
        grad_ref[at, :] = (do_ref[:tok, part].astype(F32) * head_share).astype(BF16)

    def put(n, block):
        start = pl.multiple_of(lax.div(n, NX) * tok, tok)
        dv_ref[lax.rem(n, NX), pl.ds(start, tok), :] = block.astype(BF16)

    p_ref[last - low + 1] = jnp.zeros((tok, rows), BF16)

    def products(j, carry):
        near = low + 2 * j
        block = [chunk(n, slice(width, 2 * width)) for n in (near, jnp.minimum(near + 1, last))]
        value_t = jnp.concatenate([b.astype(F32).T.astype(BF16) for b in block], axis=1)
        weights = p_ref[pl.ds(2 * j, 2)].reshape(2 * tok, rows)
        acc_ref[...] += dot(value_t, weights, ((1,), (0,)))
        got = dot(weights, grad_ref[...], ((1,), (0,)))
        put(near, got[:tok])
        pl.when(near < last)(lambda: put(near + 1, got[tok:]))
        return carry

    lax.fori_loop(0, lax.div(last - low + 2, 2), products, 0)

    for h in range(heads):
        at = slice(h * tok, (h + 1) * tok)
        part = slice(h * width, (h + 1) * width)
        out_ref[:tok, part] = (acc_ref[:, at] * share[:, at]).T.astype(BF16)

    spare_total = group * spare
    block = extra[:, :spare, :].reshape(spare_total, 2 * width).astype(BF16)
    s = dot(block[:, :width], qs_ref[...], ((1,), (1,))) * factor
    line = lax.broadcasted_iota(jnp.int32, (spare_total, spare_heads), 0)
    column = lax.div(line, NY * spare)
    row = lax.rem(lax.div(line, spare), NY)
    key_at = (row * NX + column) * spare + lax.rem(line, spare)
    query_at = own * spare + lax.div(
        lax.broadcasted_iota(jnp.int32, (spare_total, spare_heads), 1), heads
    )
    allowed = key_at <= query_at
    s = jnp.where(allowed, s, NEG)
    p = jnp.where(allowed, jnp.exp2(s - jnp.max(s, axis=0, keepdims=True)), 0.0)
    p = (p * (1.0 / jnp.sum(p, axis=0, keepdims=True))).astype(BF16)
    outs_ref[...] = dot(p, block[:, width:], ((0,), (0,))).astype(BF16)
    got = dot(p, dos_ref[...], ((1,), (0,))).reshape(NX, NY * spare, width)
    dv_ref[:, (back + 1) * tok :, :] = got.astype(BF16)


def combine_kernel(place_ref, got_ref, hidden_ref, home_ref, mine_ref, other_ref):
    @pl.when(pl.program_id(0) == 0)
    def _():
        home_ref[...] = jnp.sum(got_ref[...].astype(F32), axis=0).astype(BF16)

    first = place_ref[2] == 0
    step, half, width = mine_ref.shape
    term = dot(hidden_ref[...], home_ref[...], ((0,), (0,))).reshape(step, NK, half, width)
    mine_ref[...] = jnp.where(first, term[:, 0], term[:, 1])
    other_ref[...] = jnp.where(first, term[:, 1], term[:, 0])


VMEM = pl.BlockSpec(memory_space=pltpu.VMEM)
SMEM = pl.BlockSpec(memory_space=pltpu.SMEM)
FULL = pltpu.CompilerParams(vmem_limit_bytes=60 * 1024 * 1024)
LIMIT = pltpu.CompilerParams(vmem_limit_bytes=50 * 1024 * 1024)


def whole(shape):
    return pl.BlockSpec(shape, lambda i: (0,) * len(shape))


def project(hidden, value_weight, keys, segment_ids):
    tok = segment_ids.shape[1]
    rows, model = hidden.shape
    width = keys.shape[1]
    steps = 5
    shape = (NY, tok // 16 + 1, 16, 2 * width)
    return pl.pallas_call(
        project_kernel,
        grid=(steps,),
        out_shape=jax.ShapeDtypeStruct(shape, BF16),
        in_specs=[
            pl.BlockSpec((rows, model // steps), lambda i: (0, i)),
            pl.BlockSpec((model // steps, width), lambda i: (i, 0)),
            whole(keys.shape),
            whole(segment_ids.shape),
        ],
        out_specs=whole(shape),
        scratch_shapes=[pltpu.VMEM((rows, width), F32)],
        compiler_params=FULL,
        name="project",
    )(hidden, value_weight, keys, segment_ids)


def select(place, got, back):
    blocks, lines, width = got.shape[1:]
    send = jax.ShapeDtypeStruct((back * (blocks - 1) + NY, lines, width), BF16)
    return pl.pallas_call(
        functools.partial(select_kernel, back=back),
        out_shape=(send,) * (NX - 1),
        in_specs=[SMEM, VMEM],
        out_specs=(VMEM,) * (NX - 1),
        compiler_params=LIMIT,
        name="select",
    )(place, got)


def attend(place, segment_ids, queries, attn_grad, spare_q, spare_do, pieces, back):
    tok = segment_ids.shape[1]
    width = spare_q.shape[1]
    heads = queries.shape[1] // width
    spare = queries.shape[0] - tok
    rows = heads * tok
    return pl.pallas_call(
        functools.partial(attend_kernel, back=back),
        out_shape=(
            jax.ShapeDtypeStruct(queries.shape, BF16),
            jax.ShapeDtypeStruct(spare_q.shape, BF16),
            jax.ShapeDtypeStruct((NX, (back + 1) * tok + NY * spare, width), BF16),
        ),
        in_specs=[SMEM] + [VMEM] * 5 + [pl.BlockSpec(memory_space=pl.ANY)] * NX,
        out_specs=(VMEM, VMEM, VMEM),
        scratch_shapes=[
            pltpu.VMEM((tok, tok), F32),
            pltpu.VMEM((8, rows), F32),
            pltpu.VMEM((8, rows), F32),
            pltpu.VMEM((8, rows), F32),
            pltpu.VMEM((8, rows), F32),
            pltpu.VMEM((width, rows), F32),
            pltpu.VMEM((back * NX + 2, tok, rows), BF16),
            pltpu.VMEM((rows, width), BF16),
            pltpu.VMEM((NX, (back + 1) * tok // 16, 16, 2 * width), BF16),
            pltpu.VMEM((NX, NY, 16, 2 * width), BF16),
            pltpu.SemaphoreType.DMA((2 * (NX - 1) + back + 2,)),
        ],
        compiler_params=LIMIT,
        name="attend",
    )(place, segment_ids, queries, attn_grad, spare_q, spare_do, *pieces)


def combine(place, got, hidden):
    rows, model = hidden.shape
    group = NY * NX
    half = model // (group * NK)
    width = got.shape[2]
    step = 4
    part = jax.ShapeDtypeStruct((group, half, width), F32)
    return pl.pallas_call(
        combine_kernel,
        grid=(group // step,),
        out_shape=(jax.ShapeDtypeStruct(got.shape[1:], BF16), part, part),
        in_specs=[
            SMEM,
            whole(got.shape),
            pl.BlockSpec((rows, model * step // group), lambda i: (0, i)),
        ],
        out_specs=(
            whole(got.shape[1:]),
            pl.BlockSpec((step, half, width), lambda i: (i, 0, 0)),
            pl.BlockSpec((step, half, width), lambda i: (i, 0, 0)),
        ),
        compiler_params=FULL,
        name="combine",
    )(place, got, hidden)


def shift(array, axis, size, step):
    return lax.ppermute(array, axis, [(i, (i + step) % size) for i in range(size)])


def body(hidden, value_weight, queries, keys, attn_grad, segment_ids, partner):
    tok = segment_ids.shape[1]
    spare = hidden.shape[0] - tok
    width = keys.shape[1]
    heads = queries.shape[1] // width
    back = MAX_SEG // (tok * NX)
    y_at, x_at, k_at = lax.axis_index("y"), lax.axis_index("x"), lax.axis_index("k")

    place = jnp.stack([y_at, x_at, k_at]).astype(jnp.int32)
    spare_q = queries[tok:].reshape(spare * heads, width)
    spare_do = attn_grad[tok:].reshape(spare * heads, width)

    column = project(hidden, value_weight, keys, segment_ids)
    column = lax.all_to_all(column, "y", 0, 0, tiled=True)
    pieces = [column]
    for s, send in enumerate(select(place, column, back)):
        pieces.append(shift(send, "x", NX, s + 1))
    main_out, spare_out, sums = attend(
        place, segment_ids, queries, attn_grad, spare_q, spare_do, pieces, back
    )

    got = lax.all_to_all(sums, "x", 0, 0, tiled=True)
    got = jnp.sum(got.astype(F32), axis=0).astype(BF16)
    main_part = got[: (back + 1) * tok].reshape(back + 1, tok, width)
    main_part = jnp.concatenate(
        [main_part, jnp.zeros((NY - back - 1, tok, width), BF16)], axis=0
    )
    main_part = jnp.concatenate([main_part, main_part], axis=0)
    main_part = lax.dynamic_slice_in_dim(main_part, (back - y_at + NY) % NY, NY, 0)
    spare_part = got[(back + 1) * tok :].reshape(NY, spare, width)
    got = lax.all_to_all(jnp.concatenate([main_part, spare_part], axis=1), "y", 0, 0, tiled=True)
    home, mine, other = combine(place, got, hidden)
    both = (mine + shift(other, "k", NK, 1)).astype(BF16)
    got = lax.all_to_all(both, ("y", "x"), 0, 0, tiled=True)
    share = jnp.sum(got.astype(F32), axis=0).astype(BF16)

    bundle = jnp.concatenate([share, home[tok:], spare_out], axis=0)
    every = lax.all_gather(bundle, ("z", "k"), axis=0)
    count = share.shape[0]
    weight_grad = jnp.sum(
        every[:, :count].astype(F32).reshape(NZ, NK * count, width), axis=0
    )
    my_partner = partner[lax.axis_index("z") * NK + k_at]
    traded = lax.dynamic_index_in_dim(every[:, count:], my_partner, 0, keepdims=False)
    attn_out = lax.dynamic_update_slice(
        main_out, traded[spare:].reshape(spare, heads * width), (tok, 0)
    )
    value_grad = jnp.concatenate([home[:tok], traded[:spare]], axis=0)
    return (attn_out, value_grad, weight_grad)


def solution(mesh):
    grid = Mesh(mesh.devices.reshape(NZ, NK, NY, NX), ("z", "k", "y", "x"))
    everywhere = P(("z", "k", "y", "x"), None)
    placed = (
        everywhere,
        P(),
        everywhere,
        everywhere,
        everywhere,
        P(("z", "k"), ("y", "x")),
        P(),
    )
    return jax.shard_map(
        body,
        mesh=grid,
        in_specs=placed,
        out_specs=(everywhere, everywhere, P(("y", "x"), None)),
        check_vma=False,
    )
```

```python
import functools
import math

import jax
import jax.numpy as jnp
from jax import lax
from jax.experimental import pallas as pl
from jax.experimental.pallas import tpu as pltpu
from jax.sharding import Mesh
from jax.sharding import PartitionSpec as P

BF16 = jnp.bfloat16
F32 = jnp.float32
NEG = -1e30
BIG = 1e30

NZ, NK, NY, NX = 12, 2, 8, 4
MAX_SEG = 4096
SAFE = 40.0
MARGIN = 1.02


def dot(a, b, dims):
    return lax.dot_general(a, b, (dims, ((), ())), preferred_element_type=F32)


def project_kernel(hidden_ref, weight_ref, keys_ref, ids_ref, main_ref, extra_ref):
    tok = main_ref.shape[0]
    width = keys_ref.shape[1]
    values = dot(hidden_ref[...], weight_ref[...], ((1,), (0,)))
    keys = keys_ref[...].astype(F32)
    ids = ids_ref[...]
    level = lax.broadcasted_iota(jnp.int32, (8, tok), 0)
    below = jnp.sum((jnp.broadcast_to(ids, (8, tok)) < level).astype(F32), axis=1, keepdims=True)
    longest = jnp.max(jnp.sum(keys * keys, axis=1, keepdims=True)) * MARGIN
    line = lax.broadcasted_iota(jnp.int32, (8, 1), 0)
    counts = jnp.broadcast_to(jnp.where(line == 4, longest, below), (8, 2 * width))
    spare = jnp.concatenate([keys[tok:], values[tok:]], axis=1)
    main_ref[...] = jnp.concatenate([keys[:tok], values[:tok]], axis=1).astype(BF16)
    extra_ref[...] = jnp.concatenate([spare, counts], axis=0).astype(BF16)


def prepare_kernel(
    place_ref,
    extra_ref,
    ids_ref,
    q_ref,
    qs_ref,
    dos_ref,
    outs_ref,
    dvs_ref,
    begin_ref,
    safe_ref,
):
    tok = ids_ref.shape[1]
    width = qs_ref.shape[1]
    heads = q_ref.shape[1] // width
    group = NY * NX
    spare_heads = qs_ref.shape[0]
    spare = spare_heads // heads
    factor = width ** (-0.5) * math.log2(math.e)
    own = place_ref[0] * NX + place_ref[1]

    extra = extra_ref[...].astype(F32).reshape(group, spare + 8, 2 * width)
    counts = jnp.sum(extra[:, spare:, :], axis=0)[:, :tok]
    ids = ids_ref[...]
    begin = jnp.zeros((1, tok), F32)
    for v in range(1, 4):
        begin = jnp.where(ids == v, counts[v : v + 1, :], begin)
    begin_ref[...] = jnp.broadcast_to(begin, begin_ref.shape)

    key_bound = jnp.max(extra[:, spare + 4, :])
    ones = jnp.ones((width, width), BF16)
    lengths = []
    for h in range(heads):
        part = q_ref[:tok, h * width : (h + 1) * width].astype(F32)
        length = dot((part * part).astype(BF16), ones, ((1,), (0,)))
        lengths.append(jnp.max(length, axis=0, keepdims=True))
    query_bound = jnp.max(jnp.concatenate(lengths, axis=0)) * MARGIN
    safe_ref[0] = (key_bound * query_bound <= SAFE * SAFE * width).astype(jnp.int32)

    spare_total = group * spare
    block = extra[:, :spare, :].reshape(spare_total, 2 * width).astype(BF16)
    s = dot(block[:, :width], qs_ref[...], ((1,), (1,))) * factor
    key_at = lax.broadcasted_iota(jnp.int32, (spare_total, spare_heads), 0)
    query_at = own * spare + lax.div(
        lax.broadcasted_iota(jnp.int32, (spare_total, spare_heads), 1), heads
    )
    allowed = key_at <= query_at
    s = jnp.where(allowed, s, NEG)
    p = jnp.where(allowed, jnp.exp2(s - jnp.max(s, axis=0, keepdims=True)), 0.0)
    p = (p * (1.0 / jnp.sum(p, axis=0, keepdims=True))).astype(BF16)
    outs_ref[...] = dot(p, block[:, width:], ((0,), (0,))).astype(BF16)
    got = dot(p, dos_ref[...], ((1,), (0,))).reshape(NY, NX, spare, width)
    for xx in range(NX):
        dvs_ref[xx] = got[:, xx].reshape(NY * spare, width).astype(BF16)


def attend_kernel(
    place_ref,
    safe_ref,
    begin_ref,
    q_ref,
    do_ref,
    dvs_ref,
    kv_ref,
    kv1_ref,
    kv2_ref,
    kv3_ref,
    out_ref,
    dv_ref,
    bias_ref,
    mask_max,
    mid_max,
    mid_shift,
    total_ref,
    acc_ref,
    p_ref,
    grad_ref,
    pack_ref,
    copy_sems,
    *,
    back,
):
    tok = begin_ref.shape[1]
    width = kv_ref.shape[1] // 2
    heads = q_ref.shape[1] // width
    rows = heads * tok
    factor = width ** (-0.5) * math.log2(math.e)
    y_at, x_at = place_ref[0], place_ref[1]
    own = y_at * NX + x_at

    copies = []
    for s, piece in enumerate((kv_ref, kv1_ref, kv2_ref, kv3_ref)):
        column = lax.rem(x_at - s + NX, NX)
        start = jnp.where((column < x_at) & (s > 0), tok, 0)
        target = pack_ref.at[column, pl.ds(pl.multiple_of(start, tok), piece.shape[0])]
        copies.append(pltpu.make_async_copy(piece, target, copy_sems.at[s]))
    for copy in copies:
        copy.start()

    dv_ref[...] = jnp.zeros_like(dv_ref)
    total_ref[...] = jnp.zeros_like(total_ref)
    acc_ref[...] = jnp.zeros_like(acc_ref)

    begin = begin_ref[0:1, :]
    first = jnp.min(begin).astype(jnp.int32)
    begin = begin.astype(jnp.int32)
    in_first = begin == first
    first_rows = jnp.concatenate([in_first] * heads, axis=1)
    safe = safe_ref[0] == 1

    base = (y_at - back) * NX
    last = back * NX + x_at
    low = jnp.maximum(first // tok - base, x_at)
    low = jnp.minimum(low, last)

    def set_bias(n):
        position = (base + n) * tok + lax.broadcasted_iota(jnp.int32, (tok, tok), 0)
        query = own * tok + lax.broadcasted_iota(jnp.int32, (tok, tok), 1)
        allowed = (position >= begin) & (position <= query)
        bias_ref[...] = jnp.where(allowed, 0.0, NEG)

    def chunk(n, part):
        start = pl.multiple_of(lax.div(n, NX) * tok, tok)
        return pack_ref[lax.rem(n, NX), pl.ds(start, tok), part]

    def scores(key_block, h):
        return dot(key_block, q_ref[:tok, h * width : (h + 1) * width], ((1,), (1,)))

    def fold(a):
        return a.reshape(tok // 8, 8, tok)

    def max_masked(n):
        set_bias(n)
        key_block = chunk(n, slice(0, width))
        for h in range(heads):
            at = slice(h * tok, (h + 1) * tok)
            s = scores(key_block, h) * factor + bias_ref[...]
            mask_max[:, at] = jnp.maximum(mask_max[:, at], jnp.max(fold(s), axis=0))

    def max_mid(n, carry):
        key_block = chunk(n, slice(0, width))
        for h in range(heads):
            at = slice(h * tok, (h + 1) * tok)
            s = scores(key_block, h)
            mid_max[:, at] = jnp.maximum(mid_max[:, at], jnp.max(fold(s), axis=0))
        return carry

    for copy in copies:
        copy.wait()

    def set_shift(top):
        mask_max[...] = jnp.broadcast_to(top, mask_max.shape)
        mid_shift[...] = jnp.broadcast_to(jnp.where(first_rows, top, BIG), mid_shift.shape)

    @pl.when(safe)
    def _():
        set_shift(jnp.zeros((1, rows), F32))

    @pl.when(jnp.logical_not(safe))
    def _():
        mask_max[...] = jnp.full_like(mask_max, NEG)
        mid_max[...] = jnp.full_like(mid_max, NEG)
        pl.when(low < last)(lambda: max_masked(low))
        lax.fori_loop(low + 1, last, max_mid, 0)
        max_masked(last)
        top = jnp.max(mask_max[...], axis=0, keepdims=True)
        mid_top = jnp.max(mid_max[...], axis=0, keepdims=True) * factor
        set_shift(jnp.where(first_rows, jnp.maximum(top, mid_top), top))

    def weigh_masked(n):
        key_block = chunk(n, slice(0, width))
        for h in range(heads):
            at = slice(h * tok, (h + 1) * tok)
            s = scores(key_block, h) * factor + bias_ref[...]
            p = jnp.exp2(s - mask_max[0:1, at])
            total_ref[:, at] += jnp.sum(fold(p), axis=0)
            p_ref[n - low, :, at] = p.astype(BF16)

    def weigh_mid(n, count):
        key_block = [chunk(n + i, slice(0, width)) for i in range(count)]
        key_block = jnp.concatenate(key_block, axis=0)
        for h in range(heads):
            at = slice(h * tok, (h + 1) * tok)
            p = jnp.exp2(scores(key_block, h) * factor - mid_shift[0:1, at])
            total_ref[:, at] += jnp.sum(p.reshape(count * tok // 8, 8, tok), axis=0)
            p_ref[pl.ds(n - low, count), :, at] = p.astype(BF16).reshape(count, tok, tok)

    def weigh_two(j, carry):
        weigh_mid(low + 1 + 2 * j, 2)
        return carry

    set_bias(last)
    weigh_masked(last)
    mid_count = jnp.maximum(last - low - 1, 0)
    lax.fori_loop(0, lax.div(mid_count, 2), weigh_two, 0)
    pl.when(lax.rem(mid_count, 2) == 1)(lambda: weigh_mid(last - 1, 1))

    @pl.when(low < last)
    def _():
        set_bias(low)
        weigh_masked(low)

    share = 1.0 / jnp.sum(total_ref[...], axis=0, keepdims=True)
    for h in range(heads):
        at = slice(h * tok, (h + 1) * tok)
        part = slice(h * width, (h + 1) * width)
        head_share = jnp.broadcast_to(share[:, at], (width, tok)).T
        grad_ref[at, :] = (do_ref[:tok, part].astype(F32) * head_share).astype(BF16)

    def put(n, block):
        start = pl.multiple_of(lax.div(n, NX) * tok, tok)
        dv_ref[lax.rem(n, NX), pl.ds(start, tok), :] = block.astype(BF16)

    p_ref[last - low + 1] = jnp.zeros((tok, rows), BF16)

    def products(j, carry):
        near = low + 2 * j
        block = [chunk(n, slice(width, 2 * width)) for n in (near, jnp.minimum(near + 1, last))]
        value_t = jnp.concatenate([b.astype(F32).T.astype(BF16) for b in block], axis=1)
        weights = p_ref[pl.ds(2 * j, 2)].reshape(2 * tok, rows)
        acc_ref[...] += dot(value_t, weights, ((1,), (0,)))
        got = dot(weights, grad_ref[...], ((1,), (0,)))
        put(near, got[:tok])
        pl.when(near < last)(lambda: put(near + 1, got[tok:]))
        return carry

    lax.fori_loop(0, lax.div(last - low + 2, 2), products, 0)

    for h in range(heads):
        at = slice(h * tok, (h + 1) * tok)
        part = slice(h * width, (h + 1) * width)
        out_ref[:tok, part] = (acc_ref[:, at] * share[:, at]).T.astype(BF16)

    dv_ref[:, (back + 1) * tok :, :] = dvs_ref[...]


def combine_kernel(place_ref, got_ref, hidden_ref, home_ref, mine_ref, other_ref):
    home = jnp.sum(got_ref[...].astype(F32), axis=0)
    home_ref[...] = home.astype(BF16)
    home = home.astype(BF16)
    first = place_ref[2] == 0
    half = mine_ref.shape[1]
    step = 4
    for c in range(0, NY * NX, step):
        columns = slice(2 * half * c, 2 * half * (c + step))
        term = dot(hidden_ref[:, columns], home, ((0,), (0,)))
        term = term.reshape(step, NK, half, home.shape[1])
        mine_ref[c : c + step] = jnp.where(first, term[:, 0], term[:, 1])
        other_ref[c : c + step] = jnp.where(first, term[:, 1], term[:, 0])


VMEM = pl.BlockSpec(memory_space=pltpu.VMEM)
SMEM = pl.BlockSpec(memory_space=pltpu.SMEM)
LIMIT = pltpu.CompilerParams(vmem_limit_bytes=50 * 1024 * 1024)


def project(hidden, value_weight, keys, segment_ids):
    tok = segment_ids.shape[1]
    width = keys.shape[1]
    return pl.pallas_call(
        project_kernel,
        out_shape=(
            jax.ShapeDtypeStruct((tok, 2 * width), BF16),
            jax.ShapeDtypeStruct((16, 2 * width), BF16),
        ),
        in_specs=[VMEM] * 4,
        out_specs=(VMEM, VMEM),
        compiler_params=LIMIT,
        name="project",
    )(hidden, value_weight, keys, segment_ids)


def prepare(place, extra, segment_ids, queries, spare_q, spare_do):
    tok = segment_ids.shape[1]
    width = spare_q.shape[1]
    spare = queries.shape[0] - tok
    return pl.pallas_call(
        prepare_kernel,
        out_shape=(
            jax.ShapeDtypeStruct(spare_q.shape, BF16),
            jax.ShapeDtypeStruct((NX, NY * spare, width), BF16),
            jax.ShapeDtypeStruct((8, tok), F32),
            jax.ShapeDtypeStruct((1,), jnp.int32),
        ),
        in_specs=[SMEM] + [VMEM] * 5,
        out_specs=(VMEM, VMEM, VMEM, SMEM),
        compiler_params=LIMIT,
        name="prepare",
    )(place, extra, segment_ids, queries, spare_q, spare_do)


def attend(place, safe, begin, queries, attn_grad, spare_sums, pieces, back):
    tok = begin.shape[1]
    width = pieces[0].shape[1] // 2
    heads = queries.shape[1] // width
    spare = queries.shape[0] - tok
    rows = heads * tok
    return pl.pallas_call(
        functools.partial(attend_kernel, back=back),
        out_shape=(
            jax.ShapeDtypeStruct(queries.shape, BF16),
            jax.ShapeDtypeStruct((NX, (back + 1) * tok + NY * spare, width), BF16),
        ),
        in_specs=[SMEM] * 2 + [VMEM] * 4 + [pl.BlockSpec(memory_space=pl.ANY)] * NX,
        out_specs=(VMEM, VMEM),
        scratch_shapes=[
            pltpu.VMEM((tok, tok), F32),
            pltpu.VMEM((8, rows), F32),
            pltpu.VMEM((8, rows), F32),
            pltpu.VMEM((8, rows), F32),
            pltpu.VMEM((8, rows), F32),
            pltpu.VMEM((width, rows), F32),
            pltpu.VMEM((back * NX + 2, tok, rows), BF16),
            pltpu.VMEM((rows, width), BF16),
            pltpu.VMEM((NX, (back + 1) * tok, 2 * width), BF16),
            pltpu.SemaphoreType.DMA((NX,)),
        ],
        compiler_params=LIMIT,
        name="attend",
    )(place, safe, begin, queries, attn_grad, spare_sums, *pieces)


def combine(place, got, hidden):
    share = hidden.shape[1] // (NY * NX * NK)
    width = got.shape[2]
    part = jax.ShapeDtypeStruct((NY * NX, share, width), F32)
    return pl.pallas_call(
        combine_kernel,
        out_shape=(jax.ShapeDtypeStruct(got.shape[1:], BF16), part, part),
        in_specs=[SMEM, VMEM, VMEM],
        out_specs=(VMEM, VMEM, VMEM),
        compiler_params=LIMIT,
        name="combine",
    )(place, got, hidden)


def shift(array, axis, size, step):
    return lax.ppermute(array, axis, [(i, (i + step) % size) for i in range(size)])


def body(hidden, value_weight, queries, keys, attn_grad, segment_ids, partner):
    tok = segment_ids.shape[1]
    spare = hidden.shape[0] - tok
    width = keys.shape[1]
    heads = queries.shape[1] // width
    back = MAX_SEG // (tok * NX)
    y_at, x_at, k_at = lax.axis_index("y"), lax.axis_index("x"), lax.axis_index("k")

    main, extra = project(hidden, value_weight, keys, segment_ids)
    spare_q = queries[tok:].reshape(spare * heads, width)
    spare_do = attn_grad[tok:].reshape(spare * heads, width)

    rows = [shift(main, "y", NY, k) for k in range(back, 0, -1)] + [main]
    extras = lax.all_to_all(
        jnp.broadcast_to(extra[None], (NY * NX,) + extra.shape), ("y", "x"), 0, 0, tiled=True
    ).reshape(NY * NX * extra.shape[0], 2 * width)
    *rows, extras = lax.optimization_barrier((*rows, extras))
    column = jnp.concatenate(rows, axis=0)
    early, late = column[: back * tok], column[tok:]
    pieces = [column]
    for s in range(1, NX):
        send = jnp.where(x_at + s < NX, late, early)
        pieces.append(shift(send, "x", NX, s))

    place = jnp.stack([y_at, x_at, k_at]).astype(jnp.int32)
    spare_out, spare_sums, begin, safe = prepare(
        place, extras, segment_ids, queries, spare_q, spare_do
    )
    main_out, sums = attend(
        place, safe, begin, queries, attn_grad, spare_sums, pieces, back
    )

    got = lax.all_to_all(sums, "x", 0, 0, tiled=True)
    got = jnp.sum(got.astype(F32), axis=0).astype(BF16)
    main_part = got[: (back + 1) * tok].reshape(back + 1, tok, width)
    main_part = jnp.concatenate(
        [main_part, jnp.zeros((NY - back - 1, tok, width), BF16)], axis=0
    )
    main_part = jnp.concatenate([main_part, main_part], axis=0)
    main_part = lax.dynamic_slice_in_dim(main_part, (back - y_at + NY) % NY, NY, 0)
    spare_part = got[(back + 1) * tok :].reshape(NY, spare, width)
    got = lax.all_to_all(jnp.concatenate([main_part, spare_part], axis=1), "y", 0, 0, tiled=True)
    home, mine, other = combine(place, got, hidden)
    both = (mine + shift(other, "k", NK, 1)).astype(BF16)
    got = lax.all_to_all(both, ("y", "x"), 0, 0, tiled=True)
    share = jnp.sum(got.astype(F32), axis=0).astype(BF16)

    bundle = jnp.concatenate([share, home[tok:], spare_out], axis=0)
    every = lax.all_gather(bundle, ("z", "k"), axis=0)
    count = share.shape[0]
    weight_grad = jnp.sum(
        every[:, :count].astype(F32).reshape(NZ, NK * count, width), axis=0
    )
    my_partner = partner[lax.axis_index("z") * NK + k_at]
    traded = lax.dynamic_index_in_dim(every[:, count:], my_partner, 0, keepdims=False)
    attn_out = lax.dynamic_update_slice(
        main_out, traded[spare:].reshape(spare, heads * width), (tok, 0)
    )
    value_grad = jnp.concatenate([home[:tok], traded[:spare]], axis=0)
    return (attn_out, value_grad, weight_grad)


def solution(mesh):
    grid = Mesh(mesh.devices.reshape(NZ, NK, NY, NX), ("z", "k", "y", "x"))
    everywhere = P(("z", "k", "y", "x"), None)
    placed = (
        everywhere,
        P(),
        everywhere,
        everywhere,
        everywhere,
        P(("z", "k"), ("y", "x")),
        P(),
    )
    return jax.shard_map(
        body,
        mesh=grid,
        in_specs=placed,
        out_specs=(everywhere, everywhere, P(("y", "x"), None)),
        check_vma=False,
    )
```

```python
import functools
import math

import jax
import jax.numpy as jnp
from jax import lax
from jax.experimental import pallas as pl
from jax.experimental.pallas import tpu as pltpu
from jax.sharding import Mesh
from jax.sharding import PartitionSpec as P

BF16 = jnp.bfloat16
F32 = jnp.float32
NEG = -1e30
BIG = 1e30

NZ, NK, NY, NX = 12, 2, 8, 4
MAX_SEG = 4096
SAFE = 40.0
MARGIN = 1.02


def dot(a, b, dims):
    return lax.dot_general(a, b, (dims, ((), ())), preferred_element_type=F32)


def project_kernel(hidden_ref, weight_ref, keys_ref, ids_ref, main_ref, extra_ref):
    tok = main_ref.shape[0]
    width = keys_ref.shape[1]
    values = dot(hidden_ref[...], weight_ref[...], ((1,), (0,)))
    keys = keys_ref[...].astype(F32)
    ids = ids_ref[...]
    level = lax.broadcasted_iota(jnp.int32, (8, tok), 0)
    below = jnp.sum((jnp.broadcast_to(ids, (8, tok)) < level).astype(F32), axis=1, keepdims=True)
    longest = jnp.max(jnp.sum(keys * keys, axis=1, keepdims=True)) * MARGIN
    line = lax.broadcasted_iota(jnp.int32, (8, 1), 0)
    counts = jnp.broadcast_to(jnp.where(line == 4, longest, below), (8, 2 * width))
    spare = jnp.concatenate([keys[tok:], values[tok:]], axis=1)
    main_ref[...] = jnp.concatenate([keys[:tok], values[:tok]], axis=1).astype(BF16)
    extra_ref[...] = jnp.concatenate([spare, counts], axis=0).astype(BF16)


def attend_kernel(
    place_ref,
    extra_ref,
    ids_ref,
    q_ref,
    do_ref,
    qs_ref,
    dos_ref,
    kv_ref,
    kv1_ref,
    kv2_ref,
    kv3_ref,
    out_ref,
    outs_ref,
    dv_ref,
    own_ref,
    bias_ref,
    mask_max,
    mid_max,
    mid_shift,
    total_ref,
    acc_ref,
    p_ref,
    grad_ref,
    pack_ref,
    copy_sems,
    *,
    back,
):
    tok = ids_ref.shape[1]
    width = kv_ref.shape[1] // 2
    heads = q_ref.shape[1] // width
    rows = heads * tok
    group = NY * NX
    spare = extra_ref.shape[0] // group - 8
    spare_heads = qs_ref.shape[0]
    factor = width ** (-0.5) * math.log2(math.e)
    y_at, x_at = place_ref[0], place_ref[1]
    own = y_at * NX + x_at

    copies = []
    for s, piece in enumerate((kv_ref, kv1_ref, kv2_ref, kv3_ref)):
        column = lax.rem(x_at - s + NX, NX)
        start = jnp.where((column < x_at) & (s > 0), tok, 0)
        target = pack_ref.at[column, pl.ds(pl.multiple_of(start, tok), piece.shape[0])]
        copies.append(pltpu.make_async_copy(piece, target, copy_sems.at[s]))
    for copy in copies:
        copy.start()

    dv_ref[...] = jnp.zeros_like(dv_ref)
    own_ref[...] = jnp.zeros_like(own_ref)
    total_ref[...] = jnp.zeros_like(total_ref)
    acc_ref[...] = jnp.zeros_like(acc_ref)

    extra = extra_ref[...].astype(F32).reshape(group, spare + 8, 2 * width)
    counts = jnp.sum(extra[:, spare:, :], axis=0)[:, :tok]
    ids = ids_ref[...]
    begin = jnp.zeros((1, tok), F32)
    for v in range(1, 4):
        begin = jnp.where(ids == v, counts[v : v + 1, :], begin)
    first = jnp.min(begin).astype(jnp.int32)
    begin = begin.astype(jnp.int32)
    in_first = begin == first
    first_rows = jnp.concatenate([in_first] * heads, axis=1)
    key_bound = jnp.max(extra[:, spare + 4, :])
    ones = jnp.ones((width, width), BF16)
    lengths = []
    for h in range(heads):
        part = q_ref[:tok, h * width : (h + 1) * width].astype(F32)
        lengths.append(jnp.max(dot((part * part).astype(BF16), ones, ((1,), (0,))), axis=0, keepdims=True))
    query_bound = jnp.max(jnp.concatenate(lengths, axis=0)) * MARGIN
    safe = key_bound * query_bound <= SAFE * SAFE * width

    base = (y_at - back) * NX
    last = back * NX + x_at
    low = jnp.maximum(first // tok - base, x_at)
    low = jnp.minimum(low, last)

    def set_bias(n):
        position = (base + n) * tok + lax.broadcasted_iota(jnp.int32, (tok, tok), 0)
        query = own * tok + lax.broadcasted_iota(jnp.int32, (tok, tok), 1)
        allowed = (position >= begin) & (position <= query)
        bias_ref[...] = jnp.where(allowed, 0.0, NEG)

    def chunk(n, part):
        start = pl.multiple_of(lax.div(n, NX) * tok, tok)
        return pack_ref[lax.rem(n, NX), pl.ds(start, tok), part]

    def scores(key_block, h):
        return dot(key_block, q_ref[:tok, h * width : (h + 1) * width], ((1,), (1,)))

    def fold(a):
        return a.reshape(tok // 8, 8, tok)

    def max_masked(n):
        set_bias(n)
        key_block = chunk(n, slice(0, width))
        for h in range(heads):
            at = slice(h * tok, (h + 1) * tok)
            s = scores(key_block, h) * factor + bias_ref[...]
            mask_max[:, at] = jnp.maximum(mask_max[:, at], jnp.max(fold(s), axis=0))

    def max_mid(n, carry):
        key_block = chunk(n, slice(0, width))
        for h in range(heads):
            at = slice(h * tok, (h + 1) * tok)
            s = scores(key_block, h)
            mid_max[:, at] = jnp.maximum(mid_max[:, at], jnp.max(fold(s), axis=0))
        return carry

    for copy in copies:
        copy.wait()

    def set_shift(top):
        mask_max[...] = jnp.broadcast_to(top, mask_max.shape)
        mid_shift[...] = jnp.broadcast_to(jnp.where(first_rows, top, BIG), mid_shift.shape)

    @pl.when(safe)
    def _():
        set_shift(jnp.zeros((1, rows), F32))

    @pl.when(jnp.logical_not(safe))
    def _():
        mask_max[...] = jnp.full_like(mask_max, NEG)
        mid_max[...] = jnp.full_like(mid_max, NEG)
        pl.when(low < last)(lambda: max_masked(low))
        lax.fori_loop(low + 1, last, max_mid, 0)
        max_masked(last)
        top = jnp.max(mask_max[...], axis=0, keepdims=True)
        mid_top = jnp.max(mid_max[...], axis=0, keepdims=True) * factor
        set_shift(jnp.where(first_rows, jnp.maximum(top, mid_top), top))

    def weigh_masked(n):
        key_block = chunk(n, slice(0, width))
        for h in range(heads):
            at = slice(h * tok, (h + 1) * tok)
            s = scores(key_block, h) * factor + bias_ref[...]
            p = jnp.exp2(s - mask_max[0:1, at])
            total_ref[:, at] += jnp.sum(fold(p), axis=0)
            p_ref[n - low, :, at] = p.astype(BF16)

    def weigh_mid(n, count):
        key_block = [chunk(n + i, slice(0, width)) for i in range(count)]
        key_block = jnp.concatenate(key_block, axis=0)
        for h in range(heads):
            at = slice(h * tok, (h + 1) * tok)
            p = jnp.exp2(scores(key_block, h) * factor - mid_shift[0:1, at])
            total_ref[:, at] += jnp.sum(p.reshape(count * tok // 8, 8, tok), axis=0)
            p_ref[pl.ds(n - low, count), :, at] = p.astype(BF16).reshape(count, tok, tok)

    def weigh_two(j, carry):
        weigh_mid(low + 1 + 2 * j, 2)
        return carry

    set_bias(last)
    weigh_masked(last)
    mid_count = jnp.maximum(last - low - 1, 0)
    lax.fori_loop(0, lax.div(mid_count, 2), weigh_two, 0)
    pl.when(lax.rem(mid_count, 2) == 1)(lambda: weigh_mid(last - 1, 1))

    @pl.when(low < last)
    def _():
        set_bias(low)
        weigh_masked(low)

    share = 1.0 / jnp.sum(total_ref[...], axis=0, keepdims=True)
    for h in range(heads):
        at = slice(h * tok, (h + 1) * tok)
        part = slice(h * width, (h + 1) * width)
        head_share = jnp.broadcast_to(share[:, at], (width, tok)).T
        grad_ref[at, :] = (do_ref[:tok, part].astype(F32) * head_share).astype(BF16)

    def put(n, block):
        column = lax.rem(n, NX)
        row = lax.div(n, NX)
        block = block.astype(BF16)

        @pl.when(column == x_at)
        def _():
            own_ref[pl.ds(pl.multiple_of(row * tok, tok), tok), :] = block

        @pl.when(column != x_at)
        def _():
            start = (row - jnp.where(column < x_at, 1, 0)) * tok
            dv_ref[column, pl.ds(pl.multiple_of(start, tok), tok), :] = block

    p_ref[last - low + 1] = jnp.zeros((tok, rows), BF16)

    def products(j, carry):
        near = low + 2 * j
        block = [chunk(n, slice(width, 2 * width)) for n in (near, jnp.minimum(near + 1, last))]
        value_t = jnp.concatenate([b.astype(F32).T.astype(BF16) for b in block], axis=1)
        weights = p_ref[pl.ds(2 * j, 2)].reshape(2 * tok, rows)
        acc_ref[...] += dot(value_t, weights, ((1,), (0,)))
        got = dot(weights, grad_ref[...], ((1,), (0,)))
        put(near, got[:tok])
        pl.when(near < last)(lambda: put(near + 1, got[tok:]))
        return carry

    lax.fori_loop(0, lax.div(last - low + 2, 2), products, 0)

    for h in range(heads):
        at = slice(h * tok, (h + 1) * tok)
        part = slice(h * width, (h + 1) * width)
        out_ref[:tok, part] = (acc_ref[:, at] * share[:, at]).T.astype(BF16)

    spare_total = group * spare
    block = extra[:, :spare, :].reshape(spare_total, 2 * width).astype(BF16)
    s = dot(block[:, :width], qs_ref[...], ((1,), (1,))) * factor
    key_at = lax.broadcasted_iota(jnp.int32, (spare_total, spare_heads), 0)
    query_at = own * spare + lax.div(
        lax.broadcasted_iota(jnp.int32, (spare_total, spare_heads), 1), heads
    )
    allowed = key_at <= query_at
    s = jnp.where(allowed, s, NEG)
    p = jnp.where(allowed, jnp.exp2(s - jnp.max(s, axis=0, keepdims=True)), 0.0)
    p = (p * (1.0 / jnp.sum(p, axis=0, keepdims=True))).astype(BF16)
    outs_ref[...] = dot(p, block[:, width:], ((0,), (0,))).astype(BF16)
    got = dot(p, dos_ref[...], ((1,), (0,))).reshape(NY, NX, spare, width)
    for xx in range(NX):
        block_sum = got[:, xx].reshape(NY * spare, width).astype(BF16)
        dv_ref[xx, back * tok :, :] = block_sum

        @pl.when(x_at == xx)
        def _(block_sum=block_sum):
            own_ref[(back + 1) * tok :, :] = block_sum


def fold_kernel(place_ref, got_ref, own_ref, out_ref, *, back):
    y_at, x_at = place_ref[0], place_ref[1]
    tok = own_ref.shape[0] - got_ref.shape[1]
    spare = (got_ref.shape[1] - back * tok) // NY
    extra = own_ref[(back + 1) * tok :, :].astype(F32)
    for xx in range(NX):
        part = got_ref[xx, back * tok :, :].astype(F32)
        extra = extra + jnp.where(x_at == xx, 0.0, part)
    for i in range(NY):
        r = lax.rem(i - y_at + back + NY, NY)
        start = pl.multiple_of(jnp.minimum(r, back) * tok, tok)
        total = own_ref[pl.ds(start, tok), :].astype(F32)
        for xx in range(NX):
            at = r - jnp.where(x_at < xx, 1, 0)
            seen = (x_at != xx) & (at >= 0) & (at < back)
            start = pl.multiple_of(jnp.clip(at, 0, back - 1) * tok, tok)
            part = got_ref[xx, pl.ds(start, tok), :].astype(F32)
            total = total + jnp.where(seen, part, 0.0)
        total = jnp.where(r <= back, total, 0.0)
        total = jnp.concatenate([total, extra[i * spare : (i + 1) * spare]], axis=0)
        out_ref[i] = total.astype(BF16)


def combine_kernel(place_ref, got_ref, hidden_ref, home_ref, mine_ref, other_ref):
    home = jnp.sum(got_ref[...].astype(F32), axis=0)
    home_ref[...] = home.astype(BF16)
    home = home.astype(BF16)
    first = place_ref[2] == 0
    half = mine_ref.shape[1]
    step = 4
    for c in range(0, NY * NX, step):
        columns = slice(2 * half * c, 2 * half * (c + step))
        term = dot(hidden_ref[:, columns], home, ((0,), (0,)))
        term = term.reshape(step, NK, half, home.shape[1])
        mine_ref[c : c + step] = jnp.where(first, term[:, 0], term[:, 1])
        other_ref[c : c + step] = jnp.where(first, term[:, 1], term[:, 0])


VMEM = pl.BlockSpec(memory_space=pltpu.VMEM)
SMEM = pl.BlockSpec(memory_space=pltpu.SMEM)
LIMIT = pltpu.CompilerParams(vmem_limit_bytes=50 * 1024 * 1024)


def project(hidden, value_weight, keys, segment_ids):
    tok = segment_ids.shape[1]
    width = keys.shape[1]
    return pl.pallas_call(
        project_kernel,
        out_shape=(
            jax.ShapeDtypeStruct((tok, 2 * width), BF16),
            jax.ShapeDtypeStruct((16, 2 * width), BF16),
        ),
        in_specs=[VMEM] * 4,
        out_specs=(VMEM, VMEM),
        compiler_params=LIMIT,
        name="project",
    )(hidden, value_weight, keys, segment_ids)


def attend(place, extra, segment_ids, queries, attn_grad, spare_q, spare_do, pieces, back):
    tok = segment_ids.shape[1]
    width = pieces[0].shape[1] // 2
    heads = queries.shape[1] // width
    spare = extra.shape[0] // (NY * NX) - 8
    rows = heads * tok
    return pl.pallas_call(
        functools.partial(attend_kernel, back=back),
        out_shape=(
            jax.ShapeDtypeStruct(queries.shape, BF16),
            jax.ShapeDtypeStruct(spare_q.shape, BF16),
            jax.ShapeDtypeStruct((NX, back * tok + NY * spare, width), BF16),
            jax.ShapeDtypeStruct(((back + 1) * tok + NY * spare, width), BF16),
        ),
        in_specs=[SMEM] + [VMEM] * 6 + [pl.BlockSpec(memory_space=pl.ANY)] * NX,
        out_specs=(VMEM,) * 4,
        scratch_shapes=[
            pltpu.VMEM((tok, tok), F32),
            pltpu.VMEM((8, rows), F32),
            pltpu.VMEM((8, rows), F32),
            pltpu.VMEM((8, rows), F32),
            pltpu.VMEM((8, rows), F32),
            pltpu.VMEM((width, rows), F32),
            pltpu.VMEM((back * NX + 2, tok, rows), BF16),
            pltpu.VMEM((rows, width), BF16),
            pltpu.VMEM((NX, (back + 1) * tok, 2 * width), BF16),
            pltpu.SemaphoreType.DMA((NX,)),
        ],
        compiler_params=LIMIT,
        name="attend",
    )(place, extra, segment_ids, queries, attn_grad, spare_q, spare_do, *pieces)


def fold(place, got, own, tok, back):
    spare = (got.shape[1] - back * tok) // NY
    return pl.pallas_call(
        functools.partial(fold_kernel, back=back),
        out_shape=jax.ShapeDtypeStruct((NY, tok + spare, got.shape[2]), BF16),
        in_specs=[SMEM, VMEM, VMEM],
        out_specs=VMEM,
        compiler_params=LIMIT,
        name="fold",
    )(place, got, own)


def combine(place, got, hidden):
    share = hidden.shape[1] // (NY * NX * NK)
    width = got.shape[2]
    part = jax.ShapeDtypeStruct((NY * NX, share, width), F32)
    return pl.pallas_call(
        combine_kernel,
        out_shape=(jax.ShapeDtypeStruct(got.shape[1:], BF16), part, part),
        in_specs=[SMEM, VMEM, VMEM],
        out_specs=(VMEM, VMEM, VMEM),
        compiler_params=LIMIT,
        name="combine",
    )(place, got, hidden)


def shift(array, axis, size, step):
    return lax.ppermute(array, axis, [(i, (i + step) % size) for i in range(size)])


def body(hidden, value_weight, queries, keys, attn_grad, segment_ids, partner):
    tok = segment_ids.shape[1]
    spare = hidden.shape[0] - tok
    width = keys.shape[1]
    heads = queries.shape[1] // width
    back = MAX_SEG // (tok * NX)
    y_at, x_at, k_at = lax.axis_index("y"), lax.axis_index("x"), lax.axis_index("k")

    main, extra = project(hidden, value_weight, keys, segment_ids)
    spare_q = queries[tok:].reshape(spare * heads, width)
    spare_do = attn_grad[tok:].reshape(spare * heads, width)

    rows = [shift(main, "y", NY, k) for k in range(back, 0, -1)] + [main]
    extras = lax.all_to_all(
        jnp.broadcast_to(extra[None], (NY * NX,) + extra.shape), ("y", "x"), 0, 0, tiled=True
    ).reshape(NY * NX * extra.shape[0], 2 * width)
    column = jnp.concatenate(rows, axis=0)
    early, late = column[: back * tok], column[tok:]
    pieces = [column]
    for s in range(1, NX):
        send = jnp.where(x_at + s < NX, late, early)
        pieces.append(shift(send, "x", NX, s))

    place = jnp.stack([y_at, x_at, k_at]).astype(jnp.int32)
    main_out, spare_out, sums, own_sums = attend(
        place, extras, segment_ids, queries, attn_grad, spare_q, spare_do, pieces, back
    )

    got = lax.all_to_all(sums, "x", 0, 0, tiled=True)
    got = lax.all_to_all(fold(place, got, own_sums, tok, back), "y", 0, 0, tiled=True)
    home, mine, other = combine(place, got, hidden)
    both = (mine + shift(other, "k", NK, 1)).astype(BF16)
    got = lax.all_to_all(both, ("y", "x"), 0, 0, tiled=True)
    share = jnp.sum(got.astype(F32), axis=0).astype(BF16)

    bundle = jnp.concatenate([share, home[tok:], spare_out], axis=0)
    every = lax.all_gather(bundle, ("z", "k"), axis=0)
    count = share.shape[0]
    weight_grad = jnp.sum(
        every[:, :count].astype(F32).reshape(NZ, NK * count, width), axis=0
    )
    my_partner = partner[lax.axis_index("z") * NK + k_at]
    traded = lax.dynamic_index_in_dim(every[:, count:], my_partner, 0, keepdims=False)
    attn_out = lax.dynamic_update_slice(
        main_out, traded[spare:].reshape(spare, heads * width), (tok, 0)
    )
    value_grad = jnp.concatenate([home[:tok], traded[:spare]], axis=0)
    return (attn_out, value_grad, weight_grad)


def solution(mesh):
    grid = Mesh(mesh.devices.reshape(NZ, NK, NY, NX), ("z", "k", "y", "x"))
    everywhere = P(("z", "k", "y", "x"), None)
    placed = (
        everywhere,
        P(),
        everywhere,
        everywhere,
        everywhere,
        P(("z", "k"), ("y", "x")),
        P(),
    )
    return jax.shard_map(
        body,
        mesh=grid,
        in_specs=placed,
        out_specs=(everywhere, everywhere, P(("y", "x"), None)),
        check_vma=False,
    )
```
